768 devices in a mesh: tensor: 32 (over x, y), contract: 24 (over z, core).
Axes of the slice: x: 4, y: 8, z: 12, core: 2. Of those that a mesh axis runs over, the one named last changes fastest.
Arguments:
- amplitudes: bfloat16 [32, 12, 96, 3072], P('tensor', None, None, 'contract'), may hold values from -6 to 6
- pair_mask: int32 [32, 12], P('tensor'), may hold values 0 or 1
- tile_mask: int32 [24], replicated, may hold values 0 or 1
- cycle_integrals: bfloat16 [12, 3072, 12, 128], P(None, 'contract'), may hold values from -0.03125 to 0.03125
- ladder_integrals: bfloat16 [8, 3072, 96, 128], P(None, 'contract', None, 'tensor'), may hold values from -0.0390625 to 0.0390625
Outputs:
- residual: bfloat16 [32, 12, 96, 128], P('tensor', None, 'contract')
The draws below stay inside these ranges and needn't reach their ends.
All inputs are finite; a program needn't handle non-finite values. No bound on the sum of `pair_mask` on one device may be relied on, other than what follows from the above.
Results may differ from the reference program's by a relative error of at most 0.0013.
Values may be sent and summed in bfloat16 or wider, within the bound.
A program may use at most 64 MiB of HBM per device.

```python
import jax
import jax.numpy as jnp
from jax import lax

TILE = 128
OJ = 12
CW = 8
OI = 32
WA = 96
V = 3072
VT = 24
N_CONTRACT = 24


def plant(values, key, smallest, top_value):
    longest = values.shape.index(max(values.shape))
    spots = []
    for shift in (0, 1):
        where = [jax.random.randint(jax.random.fold_in(key, axis), (), 0, length) for axis, length in enumerate(values.shape)]
        where[longest] = (where[longest] + shift) % values.shape[longest]
        spots.append(tuple(where))
    return values.at[spots[0]].set(smallest).at[spots[1]].set(top_value)


def block_levels(key, extent, cuts, least, high):
    loudness, own = 1.0, jax.random.fold_in(key, 6)
    for dim, parts in cuts:
        heights = jnp.exp(jax.random.uniform(jax.random.fold_in(own, dim), (parts,), jnp.float32, least / len(cuts), high / len(cuts)))
        loudness = loudness * jnp.repeat(heights, extent[dim] // parts).reshape([-1 if axis == dim else 1 for axis in range(len(extent))])
    return loudness


def centred(own_key, dims, deviation, reach, cuts=(), kind=jnp.bfloat16):
    values = jax.random.normal(own_key, dims, jnp.float32) * deviation
    if len(cuts) > 0:
        values = block_levels(own_key, dims, cuts, -0.22, 0.18) * values
    return jnp.clip(values, min=-reach, max=reach).astype(kind)


def setup_inputs(seed: int = 0) -> dict:
    key_list = jax.random.split(jax.random.key(seed), 6)
    return {
        "amplitudes": centred(key_list[0], (OI, OJ, WA, V), 1.0, 6.0, ((0, 32), (3, 24))),
        "pair_mask": plant((jax.random.randint(key_list[1], (OI, OJ), 0, 4) < 3).astype(jnp.int32), jax.random.fold_in(key_list[1], 1), 0, 1),
        "tile_mask": plant((jax.random.randint(key_list[2], (VT,), 0, 4) < 3).astype(jnp.int32), jax.random.fold_in(key_list[2], 1), 0, 1),
        "cycle_integrals": centred(key_list[3], (OJ, V, OJ, TILE), (OJ * V) ** -0.5, 0.03125, ((1, 24),)),
        "ladder_integrals": centred(key_list[4], (CW, V, WA, TILE), (CW * V) ** -0.5, 0.0390625, ((1, 24), (3, 32))),
    }


def reference(amplitudes, pair_mask, tile_mask, cycle_integrals, ladder_integrals):
    masked = amplitudes * pair_mask[:, :, None, None].astype(amplitudes.dtype)

    def section_step(section, totals):
        ladder_acc, cycle_acc = totals
        index = jnp.asarray(section).astype(jnp.int32)
        offset = (index * TILE).astype(jnp.int32)
        section_block = lax.dynamic_slice_in_dim(masked, offset, TILE, 3)
        kept_tile = lax.dynamic_index_in_dim(tile_mask, index, 0, keepdims=False).astype(ladder_integrals.dtype)
        integral_block = lax.dynamic_slice_in_dim(ladder_integrals, offset, TILE, 1) * kept_tile
        ladder_left = section_block[:, :, :CW, :].reshape(OI * OJ, CW * TILE)
        ladder_acc = ladder_acc + jnp.dot(ladder_left, integral_block.reshape(CW * TILE, WA * TILE), preferred_element_type=jnp.float32)
        cycle_left = jnp.transpose(section_block, (0, 2, 1, 3)).reshape(OI * WA, OJ * TILE)
        cycle_right = lax.dynamic_slice_in_dim(cycle_integrals, offset, TILE, 1).reshape(OJ * TILE, OJ * TILE)
        cycle_acc = cycle_acc + jnp.dot(cycle_left, cycle_right, preferred_element_type=jnp.float32)
        return ladder_acc, cycle_acc

    start = (jnp.zeros((OI * OJ, WA * TILE), jnp.float32), jnp.zeros((OI * WA, OJ * TILE), jnp.float32))
    ladder, cycle = lax.fori_loop(0, N_CONTRACT, section_step, start)
    cycle = jnp.transpose(cycle.reshape(OI, WA, OJ, TILE), (0, 2, 1, 3))
    return (ladder.reshape(OI, OJ, WA, TILE) + cycle).astype(jnp.bfloat16)
```

```python
import jax
import jax.numpy as jnp
from jax import lax
from jax.experimental import pallas as pl
from jax.experimental.pallas import tpu as pltpu
from jax.sharding import PartitionSpec as P

X, Y, Z = 4, 8, 12
PLANE = X * Y
J, WIN, TILE, CW, AB = 12, 96, 128, 8, 384
MESH = pl.DeviceIdType.MESH
F32, BF16 = jnp.float32, jnp.bfloat16
Y_FAR = (4, 3, 5, 2, 6, 1, 7)
Y_NEAR = Y_FAR[::-1]
X_FAR = (2, 1, 3)
Z_FAR = (6, 5, 7, 4, 8, 3, 9, 2, 10, 1, 11)


def kernel(
    pm, tm, a_hbm, w_hbm, g_hbm, out,
    av, am, wv, gv, ag, mf, rhs, pc, rc, zc, pz, rz, zr, r1, w2, w3, zz,
    load_sem, w_sem, ag_s, ag_r, x_s, x_r, zc_s, zc_r, zl_s, zl_r, a2a_s, a2a_r, self_sem,
):
    t = lax.axis_index("tensor")
    s = lax.axis_index("contract")
    x, y, z, c = t // Y, t % Y, s // 2, s % 2

    def plane(dx, dy):
        return {"tensor": lax.rem(x + dx + X, X) * Y + lax.rem(y + dy + Y, Y), "contract": s}

    def column(dz):
        return {"tensor": t, "contract": lax.rem(z + dz + Z, Z) * 2 + c}

    sibling = {"tensor": t, "contract": z * 2 + 1 - c}

    def remote(src, dst, ss, rs, to):
        return pltpu.make_async_remote_copy(
            src_ref=src, dst_ref=dst, send_sem=ss, recv_sem=rs, device_id=to, device_id_type=MESH
        )

    load_a = pltpu.make_async_copy(a_hbm, av, load_sem.at[0])
    load_a.start()
    barrier = pltpu.get_barrier_semaphore()
    others = [(dx, dy) for dx in range(X) for dy in range(Y) if (dx, dy) != (0, 0)]
    for dx, dy in others:
        pl.semaphore_signal(barrier, inc=1, device_id=plane(dx, dy), device_id_type=MESH)
    for dz in Z_FAR:
        pl.semaphore_signal(barrier, inc=1, device_id=column(dz), device_id_type=MESH)
    pl.semaphore_signal(barrier, inc=1, device_id=sibling, device_id_type=MESH)
    load_w = [
        pltpu.make_async_copy(w_hbm.at[:, 2 * q : 2 * q + 2], wv.at[:, 2 * q : 2 * q + 2], w_sem.at[q])
        for q in range(J // 2)
    ]
    for copy in load_w:
        copy.start()
    load_g = [
        pltpu.make_async_copy(g_hbm.at[k], gv.at[:, k * TILE : (k + 1) * TILE], load_sem.at[1 + k])
        for k in range(CW)
    ]
    for copy in load_g:
        copy.start()

    load_a.wait()
    kept = tm[0, s].astype(F32)
    for j in range(J):
        m = pm[0, j].astype(F32)
        ag[0, j * CW : (j + 1) * CW, :] = (av[j, :CW, :].astype(F32) * (m * kept)).astype(BF16)
    pl.semaphore_wait(barrier, len(others) + len(Z_FAR) + 1)

    def gather(dy, dx, src, to):
        slot = dy * X + dx
        return remote(src, ag.at[slot], ag_s.at[slot], ag_r.at[slot], to)

    gathers = []
    for dy in Y_FAR:
        gathers.append(gather(dy, 0, ag.at[0], plane(0, -dy)))
    for dx in X_FAR:
        gathers.append(gather(0, dx, ag.at[0], plane(-dx, 0)))
    for copy in gathers:
        copy.start()

    def place(slot):
        il = slot
        block = ag[slot].astype(F32)
        for j in range(J):
            mf[pl.ds(j * PLANE + il, CW, stride=AB), :] = block[j * CW : (j + 1) * CW, :]

    for j in range(J):
        m = pm[0, j].astype(F32)
        am[:, j * TILE : (j + 1) * TILE] = (av[j].astype(F32) * m).astype(BF16)
    left = am[...]
    for q in range(J // 2):
        load_w[q].wait()
        right = jnp.concatenate(
            [wv[:, 2 * q + h].reshape(J * TILE, TILE) for h in range(2)], axis=1
        )
        product = jnp.dot(left, right, preferred_element_type=F32)
        for zd in range(Z):
            for cd in range(2):
                rows = product[zd * 8 + cd * 4 : zd * 8 + cd * 4 + 4, :]
                pc[cd, zd, 8 * q : 8 * q + 8, :] = jnp.concatenate([rows[:, :TILE], rows[:, TILE:]], axis=0)
    cycle_swap = remote(pc.at[1 - c], rc, x_s.at[0], x_r.at[0], sibling)
    cycle_swap.start()

    for dy in Y_NEAR:
        gather(dy, 0, ag.at[0], plane(0, -dy)).wait_recv()
        for dx in X_FAR:
            copy = gather(dy, dx, ag.at[dy * X], plane(-dx, 0))
            copy.start()
            gathers.append(copy)

    cycle_swap.wait()
    cycle_sends = []
    rc[...] = rc[...] + pc[c]
    for dz in Z_FAR:
        copy = remote(rc.at[lax.rem(z + Z - dz, Z)], zc.at[dz - 1], zc_s.at[dz - 1], zc_r.at[dz - 1], column(-dz))
        copy.start()
        cycle_sends.append(copy)

    place(0)
    for dy in Y_NEAR:
        place(dy * X)
    for dy in (0,) + Y_NEAR:
        for dx in (1, 3, 2):
            gather(dy, dx, ag.at[0], plane(-dx, 0)).wait_recv()
            place(dy * X + dx)
    for k in range(CW):
        rhs[:, k * TILE : (k + 1) * TILE] = mf[k * AB : (k + 1) * AB, :].astype(BF16)
    for copy in load_g:
        copy.wait()
    ladder = lax.dot_general(gv[...], rhs[...], (((1,), (1,)), ((), ())), preferred_element_type=F32)
    for zd in range(Z):
        for cd in range(2):
            row = zd * 32 + cd * 16
            pz[cd, zd] = ladder[row : row + 16, :]
    ladder_swap = remote(pz.at[1 - c], rz, x_s.at[1], x_r.at[1], sibling)
    ladder_swap.start()
    ladder_swap.wait()
    rz[...] = rz[...] + pz[c]
    ladder_sends = []
    for dz in Z_FAR:
        copy = remote(rz.at[lax.rem(z + Z - dz, Z)], zr.at[dz - 1], zl_s.at[dz - 1], zl_r.at[dz - 1], column(-dz))
        copy.start()
        ladder_sends.append(copy)

    cycle = rc[z]
    for dz in range(1, Z):
        remote(rc.at[0], zc.at[dz - 1], zc_s.at[dz - 1], zc_r.at[dz - 1], column(-dz)).wait_recv()
        cycle = cycle + zc[dz - 1]

    total = rz[z]
    for dz in (1, 11, 2, 10, 3, 9, 4, 8, 5, 7, 6):
        remote(rz.at[0], zr.at[dz - 1], zl_s.at[dz - 1], zl_r.at[dz - 1], column(-dz)).wait_recv()
        total = total + zr[dz - 1]
    for k in range(3):
        r1[16 * k : 16 * k + 16, :] = total[:, k * TILE : (k + 1) * TILE]
    flipped = jnp.concatenate(
        [
            jnp.transpose(jnp.concatenate([r1[pl.ds(16 * k + b, 4, stride=4), :] for b in range(4)], axis=0))
            for k in range(3)
        ],
        axis=0,
    )
    lane = lax.broadcasted_iota(jnp.int32, (PLANE, TILE), 1)
    pieces = [jnp.zeros((PLANE, TILE), F32) for _ in range(4)]
    for j in range(J):
        block = jnp.concatenate(
            [flipped[j * PLANE : (j + 1) * PLANE, :], jnp.zeros((PLANE, TILE - 16), F32)], axis=1
        )
        block = pltpu.roll(block, 4 * j, 1)
        for b in range(4):
            low = 4 * (j + b)
            pieces[b] = jnp.where((lane >= low) & (lane < low + 4), block, pieces[b])
    for b in range(4):
        piece = pieces[b] if b == 0 else pltpu.roll(pieces[b], TILE - 4 * b, 1)
        w2[pl.ds(b, PLANE, stride=4), :] = piece
    w3[...] = w2[...].reshape(PLANE, 4, TILE)
    own = pltpu.make_async_copy(w3.at[0], zz.at[t], self_sem)
    own.start()
    blocks = []
    for dx, dy in sorted(others, key=lambda o: -min(o[0], X - o[0]) - min(o[1], Y - o[1])):
        slot = dy * X + dx
        copy = remote(w3.at[slot], zz.at[t], a2a_s.at[slot], a2a_r.at[t], plane(dx, dy))
        copy.start()
        blocks.append(copy)
    own.wait()
    for dx, dy in others:
        src = plane(dx, dy)["tensor"]
        remote(w3.at[0], zz.at[src], a2a_s.at[0], a2a_r.at[src], plane(dx, dy)).wait_recv()
    final = jnp.transpose(zz[...].reshape(PLANE * 4, TILE))
    out[...] = (final[: J * 4, :] + cycle).astype(BF16)
    for copy in gathers + cycle_sends + ladder_sends + blocks:
        copy.wait_send()


def body(amplitudes, pair_mask, tile_mask, cycle_integrals, ladder_integrals):
    w = jnp.transpose(cycle_integrals, (0, 2, 1, 3))
    g = jnp.transpose(ladder_integrals, (0, 2, 3, 1)).reshape(CW, AB, TILE)
    smem = pl.BlockSpec(memory_space=pltpu.SMEM)
    anywhere = pl.BlockSpec(memory_space=pl.ANY)
    dma = pltpu.SemaphoreType.DMA
    out = pl.pallas_call(
        kernel,
        out_shape=jax.ShapeDtypeStruct((J * 4, TILE), BF16),
        in_specs=[smem, smem, anywhere, anywhere, anywhere],
        out_specs=pl.BlockSpec(memory_space=pltpu.VMEM),
        scratch_shapes=[
            pltpu.VMEM((J, WIN, TILE), BF16),
            pltpu.VMEM((WIN, J * TILE), BF16),
            pltpu.VMEM((J, J, TILE, TILE), BF16),
            pltpu.VMEM((AB, CW * TILE), BF16),
            pltpu.VMEM((PLANE, J * CW, TILE), BF16),
            pltpu.VMEM((CW * AB, TILE), F32),
            pltpu.VMEM((AB, CW * TILE), BF16),
            pltpu.VMEM((2, Z, J * 4, TILE), F32),
            pltpu.VMEM((Z, J * 4, TILE), F32),
            pltpu.VMEM((Z - 1, J * 4, TILE), F32),
            pltpu.VMEM((2, Z, 16, AB), F32),
            pltpu.VMEM((Z, 16, AB), F32),
            pltpu.VMEM((Z - 1, 16, AB), F32),
            pltpu.VMEM((48, TILE), F32),
            pltpu.VMEM((PLANE * 4, TILE), F32),
            pltpu.VMEM((PLANE, 4, TILE), F32),
            pltpu.VMEM((PLANE, 4, TILE), F32),
            dma((1 + CW,)), dma((J // 2,)), dma((PLANE,)), dma((PLANE,)), dma((2,)), dma((2,)),
            dma((Z - 1,)), dma((Z - 1,)), dma((Z - 1,)), dma((Z - 1,)), dma((PLANE,)), dma((PLANE,)),
            dma,
        ],
        compiler_params=pltpu.CompilerParams(
            collective_id=0, has_side_effects=True, vmem_limit_bytes=60 * 2**20
        ),
    )(pair_mask, tile_mask.reshape(1, -1), amplitudes[0], w, g)
    return out.reshape(1, J, 4, TILE)


def solution(mesh):
    in_specs = (
        P("tensor", None, None, "contract"),
        P("tensor", None),
        P(),
        P(None, "contract", None, None),
        P(None, "contract", None, "tensor"),
    )
    out_specs = P("tensor", None, "contract", None)
    return jax.shard_map(body, mesh=mesh, in_specs=in_specs, out_specs=out_specs, check_vma=False)
```

```python
import jax
import jax.numpy as jnp
from jax import lax
from jax.experimental import pallas as pl
from jax.experimental.pallas import tpu as pltpu
from jax.sharding import PartitionSpec as P

X, Y, Z = 4, 8, 12
PLANE = X * Y
J, WIN, TILE, CW, AB = 12, 96, 128, 8, 384
MESH = pl.DeviceIdType.MESH
F32, BF16 = jnp.float32, jnp.bfloat16
Y_FAR = (4, 3, 5, 2, 6, 1, 7)
X_FAR = (2, 1, 3)
GI = 16
GC = J * GI
GROUPS = tuple(
    tuple((dy, dx) for dy in rows for dx in (0, 1, 3, 2)) for rows in ((0, 1, 7, 2), (6, 3, 5, 4))
)
Z_FAR = (6, 5, 7, 4, 8, 3, 9, 2, 10, 1, 11)


def hops(slot):
    dy, dx = slot
    return min(dy, Y - dy) + min(dx, X - dx)


def kernel(
    pm, tm, a_hbm, w_hbm, g_hbm, out,
    av, am, wv, gv, ag, mf, rhs, pc, rc, zc, pz, rz, zr, r1, w2, w3, zz,
    load_sem, w_sem, ag_s, ag_r, x_s, x_r, zc_s, zc_r, zl_s, zl_r, a2a_s, a2a_r, self_sem,
):
    t = lax.axis_index("tensor")
    s = lax.axis_index("contract")
    x, y, z, c = t // Y, t % Y, s // 2, s % 2

    def plane(dx, dy):
        return {"tensor": lax.rem(x + dx + X, X) * Y + lax.rem(y + dy + Y, Y), "contract": s}

    def column(dz):
        return {"tensor": t, "contract": lax.rem(z + dz + Z, Z) * 2 + c}

    sibling = {"tensor": t, "contract": z * 2 + 1 - c}

    def remote(src, dst, ss, rs, to):
        return pltpu.make_async_remote_copy(
            src_ref=src, dst_ref=dst, send_sem=ss, recv_sem=rs, device_id=to, device_id_type=MESH
        )

    barrier = pltpu.get_barrier_semaphore()
    others = [(dx, dy) for dx in range(X) for dy in range(Y) if (dx, dy) != (0, 0)]
    line = [plane(dx, dy) for dx, dy in others if 0 in (dx, dy)]
    line += [column(dz) for dz in Z_FAR] + [sibling]
    for peer in line:
        pl.semaphore_signal(barrier, inc=1, device_id=peer, device_id_type=MESH)
    load_a = pltpu.make_async_copy(a_hbm, av, load_sem.at[0])
    load_a.start()
    load_w = [
        pltpu.make_async_copy(w_hbm.at[:, 2 * q : 2 * q + 2], wv.at[:, 2 * q : 2 * q + 2], w_sem.at[q])
        for q in range(J // 2)
    ]
    for copy in load_w:
        copy.start()
    load_g = [
        pltpu.make_async_copy(g_hbm.at[k], gv.at[:, k * TILE : (k + 1) * TILE], load_sem.at[1 + k])
        for k in range(CW)
    ]
    for copy in load_g:
        copy.start()

    load_a.wait()
    kept = tm[0, s].astype(F32)
    for j in range(J):
        m = pm[0, j].astype(F32)
        ag[0, j * CW : (j + 1) * CW, :] = (av[j, :CW, :].astype(F32) * (m * kept)).astype(BF16)
    pl.semaphore_wait(barrier, len(line))

    def gather(dy, dx, src, to):
        slot = dy * X + dx
        return remote(src, ag.at[slot], ag_s.at[slot], ag_r.at[slot], to)

    gathers = []
    for dy in Y_FAR:
        gathers.append(gather(dy, 0, ag.at[0], plane(0, -dy)))
    for dx in X_FAR:
        gathers.append(gather(0, dx, ag.at[0], plane(-dx, 0)))
    for copy in gathers:
        copy.start()

    def place(group, il):
        dy, dx = GROUPS[group][il]
        block = ag[dy * X + dx].astype(F32)
        for j in range(J):
            mf[group, pl.ds(j * GI + il, CW, stride=GC), :] = block[j * CW : (j + 1) * CW, :]

    for j in range(J):
        m = pm[0, j].astype(F32)
        am[:, j * TILE : (j + 1) * TILE] = (av[j].astype(F32) * m).astype(BF16)
    left = am[...]
    for q in range(J // 2):
        load_w[q].wait()
        right = jnp.concatenate(
            [wv[:, 2 * q + h].reshape(J * TILE, TILE) for h in range(2)], axis=1
        )
        product = jnp.dot(left, right, preferred_element_type=F32)
        for zd in range(Z):
            for cd in range(2):
                rows = product[zd * 8 + cd * 4 : zd * 8 + cd * 4 + 4, :]
                pc[cd, zd, 8 * q : 8 * q + 8, :] = jnp.concatenate([rows[:, :TILE], rows[:, TILE:]], axis=0)
    cycle_swap = remote(pc.at[1 - c], rc, x_s.at[0], x_r.at[0], sibling)
    cycle_swap.start()

    for dx in (1, 3, 2):
        gather(0, dx, ag.at[0], plane(-dx, 0)).wait_recv()
        for dy in (1, 7):
            copy = gather(dy, dx, ag.at[dx], plane(0, -dy))
            copy.start()
            gathers.append(copy)
    for dy in (2, 6, 3, 5, 4):
        gather(dy, 0, ag.at[0], plane(0, -dy)).wait_recv()
        for dx in X_FAR:
            copy = gather(dy, dx, ag.at[dy * X], plane(-dx, 0))
            copy.start()
            gathers.append(copy)
    for dy in (1, 7):
        gather(dy, 0, ag.at[0], plane(0, -dy)).wait_recv()

    cycle_swap.wait()
    cycle_sends = []
    rc[...] = rc[...] + pc[c]
    for dz in Z_FAR:
        copy = remote(rc.at[lax.rem(z + Z - dz, Z)], zc.at[dz - 1], zc_s.at[dz - 1], zc_r.at[dz - 1], column(-dz))
        copy.start()
        cycle_sends.append(copy)

    for copy in load_g:
        copy.wait()
    swaps, ladder_sends = [], []

    def pick(group, ils):
        for il in ils:
            dy, dx = GROUPS[group][il]
            if dx:
                if dy:
                    gather(dy, dx, ag.at[0], plane(-dx, 0)).wait_recv()
            place(group, il)

    def multiply(group):
        for k in range(CW):
            rhs[group, :, k * TILE : (k + 1) * TILE] = mf[group, k * GC : (k + 1) * GC, :].astype(BF16)
        ladder = lax.dot_general(
            gv[...], rhs[group], (((1,), (1,)), ((), ())), preferred_element_type=F32
        )
        for zd in range(Z):
            for cd in range(2):
                rows = ladder[zd * 32 + cd * 16 : zd * 32 + cd * 16 + 16, :]
                pz[group, cd, zd, :16, :] = rows[:, :TILE]
                pz[group, cd, zd, 16:, :] = jnp.concatenate([rows[:8, TILE:], rows[8:, TILE:]], axis=1)
        swap = remote(pz.at[group, 1 - c], rz.at[group], x_s.at[1 + group], x_r.at[1 + group], sibling)
        swap.start()
        swaps.append(swap)

    def scatter(group):
        swaps[group].wait()
        rz[group] = rz[group] + pz[group, c]
        for dz in Z_FAR:
            copy = remote(
                rz.at[group, lax.rem(z + Z - dz, Z)], zr.at[group, dz - 1],
                zl_s.at[group, dz - 1], zl_r.at[group, dz - 1], column(-dz),
            )
            copy.start()
            ladder_sends.append(copy)

    pick(0, range(GI))
    multiply(0)
    pick(1, range(4))
    scatter(0)
    pick(1, range(4, GI))
    multiply(1)
    for copy in gathers:
        copy.wait_send()
    scatter(1)

    cycle = rc[z]
    for dz in range(1, Z):
        remote(rc.at[0], zc.at[dz - 1], zc_s.at[dz - 1], zc_r.at[dz - 1], column(-dz)).wait_recv()
        cycle = cycle + zc[dz - 1]
    for copy in cycle_sends:
        copy.wait_send()

    lane = lax.broadcasted_iota(jnp.int32, (GI, TILE), 1)
    blocks = []
    for group in range(2):
        total = rz[group, z]
        for dz in (1, 11, 2, 10, 3, 9, 4, 8, 5, 7, 6):
            remote(
                rz.at[group, 0], zr.at[group, dz - 1], zl_s.at[group, dz - 1], zl_r.at[group, dz - 1], column(-dz)
            ).wait_recv()
            total = total + zr[group, dz - 1]
        r1[:24, :] = total
        r1[24:, :] = pltpu.roll(total[16:, :], 64, 1)
        flipped = jnp.concatenate(
            [
                jnp.transpose(jnp.concatenate([r1[pl.ds(16 * k + b, 4, stride=4), :] for b in range(4)], axis=0))
                for k in range(2)
            ],
            axis=0,
        )
        pieces = [jnp.zeros((GI, TILE), F32) for _ in range(4)]
        for j in range(J):
            block = jnp.concatenate(
                [flipped[j * GI : (j + 1) * GI, :], jnp.zeros((GI, TILE - 16), F32)], axis=1
            )
            block = pltpu.roll(block, 4 * j, 1)
            for b in range(4):
                low = 4 * (j + b)
                pieces[b] = jnp.where((lane >= low) & (lane < low + 4), block, pieces[b])
        for b in range(4):
            piece = pieces[b] if b == 0 else pltpu.roll(pieces[b], TILE - 4 * b, 1)
            w2[pl.ds(b, GI, stride=4), :] = piece
        w3[group] = w2[...].reshape(GI, 4, TILE)
        for il in sorted(range(GI), key=lambda il: -hops(GROUPS[group][il])):
            dy, dx = GROUPS[group][il]
            if (dy, dx) == (0, 0):
                own = pltpu.make_async_copy(w3.at[group, il], zz.at[t], self_sem)
                own.start()
                own.wait()
                continue
            slot = dy * X + dx
            copy = remote(w3.at[group, il], zz.at[t], a2a_s.at[slot], a2a_r.at[t], plane(dx, dy))
            copy.start()
            blocks.append(copy)
    for copy in ladder_sends:
        copy.wait_send()
    for dx, dy in others:
        src = plane(dx, dy)["tensor"]
        remote(w3.at[0, 0], zz.at[src], a2a_s.at[0], a2a_r.at[src], plane(dx, dy)).wait_recv()
    final = jnp.transpose(zz[...].reshape(PLANE * 4, TILE))
    out[...] = (final[: J * 4, :] + cycle).astype(BF16)
    for copy in blocks:
        copy.wait_send()


def body(amplitudes, pair_mask, tile_mask, cycle_integrals, ladder_integrals):
    w = jnp.transpose(cycle_integrals, (0, 2, 1, 3))
    g = jnp.transpose(ladder_integrals, (0, 2, 3, 1)).reshape(CW, AB, TILE)
    smem = pl.BlockSpec(memory_space=pltpu.SMEM)
    anywhere = pl.BlockSpec(memory_space=pl.ANY)
    dma = pltpu.SemaphoreType.DMA
    out = pl.pallas_call(
        kernel,
        out_shape=jax.ShapeDtypeStruct((J * 4, TILE), BF16),
        in_specs=[smem, smem, anywhere, anywhere, anywhere],
        out_specs=pl.BlockSpec(memory_space=pltpu.VMEM),
        scratch_shapes=[
            pltpu.VMEM((J, WIN, TILE), BF16),
            pltpu.VMEM((WIN, J * TILE), BF16),
            pltpu.VMEM((J, J, TILE, TILE), BF16),
            pltpu.VMEM((AB, CW * TILE), BF16),
            pltpu.VMEM((PLANE, J * CW, TILE), BF16),
            pltpu.VMEM((2, CW * GC, TILE), F32),
            pltpu.VMEM((2, GC, CW * TILE), BF16),
            pltpu.VMEM((2, Z, J * 4, TILE), F32),
            pltpu.VMEM((Z, J * 4, TILE), F32),
            pltpu.VMEM((Z - 1, J * 4, TILE), F32),
            pltpu.VMEM((2, 2, Z, 24, TILE), F32),
            pltpu.VMEM((2, Z, 24, TILE), F32),
            pltpu.VMEM((2, Z - 1, 24, TILE), F32),
            pltpu.VMEM((32, TILE), F32),
            pltpu.VMEM((GI * 4, TILE), F32),
            pltpu.VMEM((2, GI, 4, TILE), F32),
            pltpu.VMEM((PLANE, 4, TILE), F32),
            dma((1 + CW,)), dma((J // 2,)), dma((PLANE,)), dma((PLANE,)), dma((3,)), dma((3,)),
            dma((Z - 1,)), dma((Z - 1,)), dma((2, Z - 1)), dma((2, Z - 1)), dma((PLANE,)), dma((PLANE,)),
            dma,
        ],
        compiler_params=pltpu.CompilerParams(
            collective_id=0, has_side_effects=True, vmem_limit_bytes=60 * 2**20
        ),
    )(pair_mask, tile_mask.reshape(1, -1), amplitudes[0], w, g)
    return out.reshape(1, J, 4, TILE)


def solution(mesh):
    in_specs = (
        P("tensor", None, None, "contract"),
        P("tensor", None),
        P(),
        P(None, "contract", None, None),
        P(None, "contract", None, "tensor"),
    )
    out_specs = P("tensor", None, "contract", None)
    return jax.shard_map(body, mesh=mesh, in_specs=in_specs, out_specs=out_specs, check_vma=False)
```

```python
import jax
import jax.numpy as jnp
from jax import lax
from jax.experimental import pallas as pl
from jax.experimental.pallas import tpu as pltpu
from jax.sharding import PartitionSpec as P

X, Y, Z = 4, 8, 12
PLANE = X * Y
J, WIN, TILE, CW, AB = 12, 96, 128, 8, 384
MESH = pl.DeviceIdType.MESH
F32, BF16 = jnp.float32, jnp.bfloat16
Y_FAR = (4, 3, 5, 2, 6, 1, 7)
X_FAR = (2, 1, 3)
GI = 16
STEPS = 32000.0
GC = J * GI
GROUPS = tuple(
    tuple((dy, dx) for dy in rows for dx in (0, 1, 3, 2)) for rows in ((0, 1, 7, 2), (6, 3, 5, 4))
)
Z_FAR = (6, 5, 7, 4, 8, 3, 9, 2, 10, 1, 11)


def hops(slot):
    dy, dx = slot
    return min(dy, Y - dy) + min(dx, X - dx)


def encode(values):
    top = jnp.max(jnp.abs(values), axis=1, keepdims=True)
    power = jnp.ceil(jnp.log2(jnp.maximum(top, 1e-36)))
    return jnp.round(values * jnp.exp2(-power) * STEPS).astype(jnp.int32), power


def decode(code, power):
    return code * (1.0 / STEPS) * jnp.exp2(power)


def kernel(
    pm, tm, a_hbm, w_hbm, g_hbm, out,
    av, am, wv, gv, ag, mf, rhs, pc, rc, qc, ec, zc, pz, rz, qz, zr, r1, w2, w3, zz,
    load_sem, w_sem, ag_s, ag_r, x_s, x_r, zc_s, zc_r, zl_s, zl_r, a2a_s, a2a_r, self_sem,
):
    t = lax.axis_index("tensor")
    s = lax.axis_index("contract")
    x, y, z, c = t // Y, t % Y, s // 2, s % 2

    def plane(dx, dy):
        return {"tensor": lax.rem(x + dx + X, X) * Y + lax.rem(y + dy + Y, Y), "contract": s}

    def column(dz):
        return {"tensor": t, "contract": lax.rem(z + dz + Z, Z) * 2 + c}

    def target(k):
        return jnp.where(k >= z, k + 1, k)

    def place_of(zd):
        return {"tensor": t, "contract": zd * 2 + c}

    sibling = {"tensor": t, "contract": z * 2 + 1 - c}

    def remote(src, dst, ss, rs, to):
        return pltpu.make_async_remote_copy(
            src_ref=src, dst_ref=dst, send_sem=ss, recv_sem=rs, device_id=to, device_id_type=MESH
        )

    barrier = pltpu.get_barrier_semaphore()
    others = [(dx, dy) for dx in range(X) for dy in range(Y) if (dx, dy) != (0, 0)]
    line = [plane(dx, dy) for dx, dy in others if 0 in (dx, dy)]
    line += [column(dz) for dz in Z_FAR] + [sibling]
    for peer in line:
        pl.semaphore_signal(barrier, inc=1, device_id=peer, device_id_type=MESH)
    load_a = pltpu.make_async_copy(a_hbm, av, load_sem.at[0])
    load_a.start()
    load_w = [
        pltpu.make_async_copy(w_hbm.at[:, 2 * q : 2 * q + 2], wv.at[:, 2 * q : 2 * q + 2], w_sem.at[q])
        for q in range(J // 2)
    ]
    for copy in load_w:
        copy.start()
    load_g = [
        pltpu.make_async_copy(g_hbm.at[k], gv.at[:, k * TILE : (k + 1) * TILE], load_sem.at[1 + k])
        for k in range(CW)
    ]
    for copy in load_g:
        copy.start()

    load_a.wait()
    kept = tm[0, s].astype(F32)
    for j in range(J):
        m = pm[0, j].astype(F32)
        ag[0, j * CW : (j + 1) * CW, :] = (av[j, :CW, :].astype(F32) * (m * kept)).astype(BF16)
    pl.semaphore_wait(barrier, len(line))

    def gather(dy, dx, src, to):
        slot = dy * X + dx
        return remote(src, ag.at[slot], ag_s.at[slot], ag_r.at[slot], to)

    gathers = []
    for dy in Y_FAR:
        gathers.append(gather(dy, 0, ag.at[0], plane(0, -dy)))
    for dx in X_FAR:
        gathers.append(gather(0, dx, ag.at[0], plane(-dx, 0)))
    for copy in gathers:
        copy.start()

    def place(group, il):
        dy, dx = GROUPS[group][il]
        block = ag[dy * X + dx].astype(F32)
        for j in range(J):
            mf[group, pl.ds(j * GI + il, CW, stride=GC), :] = block[j * CW : (j + 1) * CW, :]

    for j in range(J):
        m = pm[0, j].astype(F32)
        am[:, j * TILE : (j + 1) * TILE] = (av[j].astype(F32) * m).astype(BF16)
    left = am[...]
    for q in range(J // 2):
        load_w[q].wait()
        right = jnp.concatenate(
            [wv[:, 2 * q + h].reshape(J * TILE, TILE) for h in range(2)], axis=1
        )
        product = jnp.dot(left, right, preferred_element_type=F32)
        for zd in range(Z):
            for cd in range(2):
                rows = product[zd * 8 + cd * 4 : zd * 8 + cd * 4 + 4, :]
                pc[cd, zd, 8 * q : 8 * q + 8, :] = jnp.concatenate([rows[:, :TILE], rows[:, TILE:]], axis=0)
    cycle_swap = remote(pc.at[1 - c], rc, x_s.at[0], x_r.at[0], sibling)
    cycle_swap.start()

    for dx in (1, 3, 2):
        gather(0, dx, ag.at[0], plane(-dx, 0)).wait_recv()
        for dy in (1, 7):
            copy = gather(dy, dx, ag.at[dx], plane(0, -dy))
            copy.start()
            gathers.append(copy)
    for dy in (2, 6, 3, 5, 4):
        gather(dy, 0, ag.at[0], plane(0, -dy)).wait_recv()
        for dx in X_FAR:
            copy = gather(dy, dx, ag.at[dy * X], plane(-dx, 0))
            copy.start()
            gathers.append(copy)
    for dy in (1, 7):
        gather(dy, 0, ag.at[0], plane(0, -dy)).wait_recv()

    cycle_swap.wait()
    cycle_sends = []
    rc[...] = rc[...] + pc[c]
    code, cycle_power = encode(rc[...])
    qc[...] = code.astype(jnp.int16)
    ec[...] = cycle_power
    for k in range(Z - 1):
        zd = target(k)
        slot = lax.rem(z - zd + Z, Z) - 1
        copy = remote(qc.at[zd], zc.at[slot], zc_s.at[k], zc_r.at[slot], place_of(zd))
        copy.start()
        cycle_sends.append(copy)

    for copy in load_g:
        copy.wait()
    swaps, ladder_sends = [], []

    def pick(group, ils):
        for il in ils:
            dy, dx = GROUPS[group][il]
            if dx:
                if dy:
                    gather(dy, dx, ag.at[0], plane(-dx, 0)).wait_recv()
            place(group, il)

    def multiply(group):
        for k in range(CW):
            rhs[group, :, k * TILE : (k + 1) * TILE] = mf[group, k * GC : (k + 1) * GC, :].astype(BF16)
        ladder = lax.dot_general(
            gv[...], rhs[group], (((1,), (1,)), ((), ())), preferred_element_type=F32
        )
        for zd in range(Z):
            for cd in range(2):
                rows = ladder[zd * 32 + cd * 16 : zd * 32 + cd * 16 + 16, :]
                pz[group, cd, zd, :16, :] = rows[:, :TILE]
                pz[group, cd, zd, 16:, :] = jnp.concatenate([rows[:8, TILE:], rows[8:, TILE:]], axis=1)
        swap = remote(pz.at[group, 1 - c], rz.at[group], x_s.at[1 + group], x_r.at[1 + group], sibling)
        swap.start()
        swaps.append(swap)

    def scatter(group):
        swaps[group].wait()
        rz[group] = rz[group] + pz[group, c]
        code, power = encode(rz[group])
        powers = [jnp.broadcast_to(p, (Z, 4, TILE)).astype(jnp.int32) for p in (power, ec[...])]
        qz[group] = jnp.concatenate([code] + powers, axis=1).astype(jnp.int16)
        for k in range(Z - 1):
            zd = target(k)
            slot = lax.rem(z - zd + Z, Z) - 1
            copy = remote(
                qz.at[group, zd], zr.at[group, slot], zl_s.at[group, k], zl_r.at[group, slot], place_of(zd)
            )
            copy.start()
            ladder_sends.append(copy)

    pick(0, range(GI))
    multiply(0)
    pick(1, range(4))
    scatter(0)
    pick(1, range(4, GI))
    multiply(1)
    for copy in gathers:
        copy.wait_send()
    scatter(1)

    cycle = rc[z]
    for dz in range(1, Z):
        remote(qc.at[0], zc.at[dz - 1], zc_s.at[0], zc_r.at[dz - 1], column(-dz)).wait_recv()
    for copy in cycle_sends:
        copy.wait_send()

    lane = lax.broadcasted_iota(jnp.int32, (GI, TILE), 1)
    blocks = []
    for group in range(2):
        total = rz[group, z]
        for dz in (1, 11, 2, 10, 3, 9, 4, 8, 5, 7, 6):
            remote(
                qz.at[group, 0], zr.at[group, dz - 1], zl_s.at[group, 0], zl_r.at[group, dz - 1], column(-dz)
            ).wait_recv()
            received = zr[group, dz - 1].astype(jnp.int32).astype(F32)
            total = total + decode(received[:24, :], received[24:25, :])
            if group == 0:
                cycle = cycle + decode(zc[dz - 1].astype(jnp.int32).astype(F32), received[28:29, :])
        r1[:24, :] = total
        r1[24:, :] = pltpu.roll(total[16:, :], 64, 1)
        flipped = jnp.concatenate(
            [
                jnp.transpose(jnp.concatenate([r1[pl.ds(16 * k + b, 4, stride=4), :] for b in range(4)], axis=0))
                for k in range(2)
            ],
            axis=0,
        )
        pieces = [jnp.zeros((GI, TILE), F32) for _ in range(4)]
        for j in range(J):
            block = jnp.concatenate(
                [flipped[j * GI : (j + 1) * GI, :], jnp.zeros((GI, TILE - 16), F32)], axis=1
            )
            block = pltpu.roll(block, 4 * j, 1)
            for b in range(4):
                low = 4 * (j + b)
                pieces[b] = jnp.where((lane >= low) & (lane < low + 4), block, pieces[b])
        for b in range(4):
            piece = pieces[b] if b == 0 else pltpu.roll(pieces[b], TILE - 4 * b, 1)
            w2[pl.ds(b, GI, stride=4), :] = piece
        w3[group] = w2[...].reshape(GI, 4, TILE)
        for il in sorted(range(GI), key=lambda il: -hops(GROUPS[group][il])):
            dy, dx = GROUPS[group][il]
            if (dy, dx) == (0, 0):
                own = pltpu.make_async_copy(w3.at[group, il], zz.at[t], self_sem)
                own.start()
                own.wait()
                continue
            slot = dy * X + dx
            copy = remote(w3.at[group, il], zz.at[t], a2a_s.at[slot], a2a_r.at[t], plane(dx, dy))
            copy.start()
            blocks.append(copy)
    for copy in ladder_sends:
        copy.wait_send()
    for dx, dy in others:
        src = plane(dx, dy)["tensor"]
        remote(w3.at[0, 0], zz.at[src], a2a_s.at[0], a2a_r.at[src], plane(dx, dy)).wait_recv()
    final = jnp.transpose(zz[...].reshape(PLANE * 4, TILE))
    out[...] = (final[: J * 4, :] + cycle).astype(BF16)
    for copy in blocks:
        copy.wait_send()


def body(amplitudes, pair_mask, tile_mask, cycle_integrals, ladder_integrals):
    w = jnp.transpose(cycle_integrals, (0, 2, 1, 3))
    g = jnp.transpose(ladder_integrals, (0, 2, 3, 1)).reshape(CW, AB, TILE)
    smem = pl.BlockSpec(memory_space=pltpu.SMEM)
    anywhere = pl.BlockSpec(memory_space=pl.ANY)
    dma = pltpu.SemaphoreType.DMA
    out = pl.pallas_call(
        kernel,
        out_shape=jax.ShapeDtypeStruct((J * 4, TILE), BF16),
        in_specs=[smem, smem, anywhere, anywhere, anywhere],
        out_specs=pl.BlockSpec(memory_space=pltpu.VMEM),
        scratch_shapes=[
            pltpu.VMEM((J, WIN, TILE), BF16),
            pltpu.VMEM((WIN, J * TILE), BF16),
            pltpu.VMEM((J, J, TILE, TILE), BF16),
            pltpu.VMEM((AB, CW * TILE), BF16),
            pltpu.VMEM((PLANE, J * CW, TILE), BF16),
            pltpu.VMEM((2, CW * GC, TILE), F32),
            pltpu.VMEM((2, GC, CW * TILE), BF16),
            pltpu.VMEM((2, Z, J * 4, TILE), F32),
            pltpu.VMEM((Z, J * 4, TILE), F32),
            pltpu.VMEM((Z, J * 4, TILE), jnp.int16),
            pltpu.VMEM((Z, 1, TILE), F32),
            pltpu.VMEM((Z - 1, J * 4, TILE), jnp.int16),
            pltpu.VMEM((2, 2, Z, 24, TILE), F32),
            pltpu.VMEM((2, Z, 24, TILE), F32),
            pltpu.VMEM((2, Z, 32, TILE), jnp.int16),
            pltpu.VMEM((2, Z - 1, 32, TILE), jnp.int16),
            pltpu.VMEM((32, TILE), F32),
            pltpu.VMEM((GI * 4, TILE), F32),
            pltpu.VMEM((2, GI, 4, TILE), F32),
            pltpu.VMEM((PLANE, 4, TILE), F32),
            dma((1 + CW,)), dma((J // 2,)), dma((PLANE,)), dma((PLANE,)), dma((3,)), dma((3,)),
            dma((Z - 1,)), dma((Z - 1,)), dma((2, Z - 1)), dma((2, Z - 1)), dma((PLANE,)), dma((PLANE,)),
            dma,
        ],
        compiler_params=pltpu.CompilerParams(
            collective_id=0, has_side_effects=True, vmem_limit_bytes=60 * 2**20
        ),
    )(pair_mask, tile_mask.reshape(1, -1), amplitudes[0], w, g)
    return out.reshape(1, J, 4, TILE)


def solution(mesh):
    in_specs = (
        P("tensor", None, None, "contract"),
        P("tensor", None),
        P(),
        P(None, "contract", None, None),
        P(None, "contract", None, "tensor"),
    )
    out_specs = P("tensor", None, "contract", None)
    return jax.shard_map(body, mesh=mesh, in_specs=in_specs, out_specs=out_specs, check_vma=False)
```

```python
import jax
import jax.numpy as jnp
from jax import lax
from jax.experimental import pallas as pl
from jax.experimental.pallas import tpu as pltpu
from jax.sharding import PartitionSpec as P

X, Y, Z = 4, 8, 12
PLANE = X * Y
J, WIN, TILE, CW, AB = 12, 96, 128, 8, 384
MESH = pl.DeviceIdType.MESH
F32, BF16 = jnp.float32, jnp.bfloat16
Y_NEAR = (2, 6, 1, 7)
X_FAR = (2, 1, 3)
GI = 16
STEPS = 32000.0
GC = J * GI
GROUPS = tuple(
    tuple((dy, dx) for dy in rows for dx in (0, 1, 3, 2)) for rows in ((0, 1, 7, 2), (6, 3, 5, 4))
)
Z_FAR = (6, 5, 7, 4, 8, 3, 9, 2, 10, 1, 11)


def hops(slot):
    dy, dx = slot
    return min(dy, Y - dy) + min(dx, X - dx)


def encode(values):
    top = jnp.max(jnp.abs(values), axis=1, keepdims=True)
    power = jnp.ceil(jnp.log2(jnp.maximum(top, 1e-36)))
    return jnp.round(values * jnp.exp2(-power) * STEPS).astype(jnp.int32), power


def decode(code, power):
    return code * (1.0 / STEPS) * jnp.exp2(power)


def kernel(
    pm, tm, a_hbm, w_hbm, g_hbm, out,
    av, am, wv, gv, ag, mf, rhs, pc, rc, qc, ec, zc, pz, rz, qz, zr, r1, w2, w3, zz,
    load_sem, w_sem, ag_s, ag_r, x_s, x_r, zc_s, zc_r, zl_s, zl_r, a2a_s, a2a_r, self_sem, known,
):
    t = lax.axis_index("tensor")
    s = lax.axis_index("contract")
    x, y, z, c = t // Y, t % Y, s // 2, s % 2

    def plane(dx, dy):
        return {"tensor": lax.rem(x + dx + X, X) * Y + lax.rem(y + dy + Y, Y), "contract": s}

    def column(dz):
        return {"tensor": t, "contract": lax.rem(z + dz + Z, Z) * 2 + c}

    def target(k):
        return jnp.where(k >= z, k + 1, k)

    def place_of(zd):
        return {"tensor": t, "contract": zd * 2 + c}

    sibling = {"tensor": t, "contract": z * 2 + 1 - c}

    def remote(src, dst, ss, rs, to):
        return pltpu.make_async_remote_copy(
            src_ref=src, dst_ref=dst, send_sem=ss, recv_sem=rs, device_id=to, device_id_type=MESH
        )

    barrier = pltpu.get_barrier_semaphore()
    others = [(dx, dy) for dx in range(X) for dy in range(Y) if (dx, dy) != (0, 0)]
    line = [plane(0, dy) for dy in Y_NEAR] + [plane(dx, 0) for dx in X_FAR]
    line += [column(1), column(-1), sibling]
    for peer in line:
        pl.semaphore_signal(barrier, inc=1, device_id=peer, device_id_type=MESH)
    load_a = pltpu.make_async_copy(a_hbm, av, load_sem.at[0])
    load_a.start()
    load_w = [
        pltpu.make_async_copy(w_hbm.at[:, 2 * q : 2 * q + 2], wv.at[:, 2 * q : 2 * q + 2], w_sem.at[q])
        for q in range(J // 2)
    ]
    for copy in load_w:
        copy.start()
    load_g = [
        pltpu.make_async_copy(g_hbm.at[k], gv.at[:, k * TILE : (k + 1) * TILE], load_sem.at[1 + k])
        for k in range(CW)
    ]
    for copy in load_g:
        copy.start()

    load_a.wait()
    kept = tm[0, s].astype(F32)
    for j in range(J):
        m = pm[0, j].astype(F32)
        ag[0, j * CW : (j + 1) * CW, :] = (av[j, :CW, :].astype(F32) * (m * kept)).astype(BF16)
    pl.semaphore_wait(barrier, len(line))

    def tell(level):
        for dz in (2**level, -(2**level)):
            pl.semaphore_signal(known.at[level], inc=1, device_id=column(dz), device_id_type=MESH)

    def hear(level):
        pl.semaphore_wait(known.at[level], 2)

    tell(0)

    def gather(dy, dx, src, to):
        slot = dy * X + dx
        return remote(src, ag.at[slot], ag_s.at[slot], ag_r.at[slot], to)

    gathers = []
    for dy in Y_NEAR:
        gathers.append(gather(dy, 0, ag.at[0], plane(0, -dy)))
    for dx in X_FAR:
        gathers.append(gather(0, dx, ag.at[0], plane(-dx, 0)))
    for copy in gathers:
        copy.start()

    def place(group, il):
        dy, dx = GROUPS[group][il]
        block = ag[dy * X + dx].astype(F32)
        for j in range(J):
            mf[group, pl.ds(j * GI + il, CW, stride=GC), :] = block[j * CW : (j + 1) * CW, :]

    for j in range(J):
        m = pm[0, j].astype(F32)
        am[:, j * TILE : (j + 1) * TILE] = (av[j].astype(F32) * m).astype(BF16)

    def cycle_product(q):
        load_w[q].wait()
        right = jnp.concatenate(
            [wv[:, 2 * q + h].reshape(J * TILE, TILE) for h in range(2)], axis=1
        )
        product = jnp.dot(am[...], right, preferred_element_type=F32)
        for zd in range(Z):
            for cd in range(2):
                rows = product[zd * 8 + cd * 4 : zd * 8 + cd * 4 + 4, :]
                pc[cd, zd, 8 * q : 8 * q + 8, :] = jnp.concatenate([rows[:, :TILE], rows[:, TILE:]], axis=0)

    def arrived(dy, dx):
        gather(dy, dx, ag.at[0], sibling).wait_recv()

    def pass_on(dy, dx, ey, ex):
        copy = gather((dy + ey) % Y, (dx + ex) % X, ag.at[dy * X + dx], plane(-ex, -ey))
        copy.start()
        gathers.append(copy)

    for q in range(3):
        cycle_product(q)
    arrived(2, 0)
    pass_on(2, 0, 1, 0)
    arrived(6, 0)
    pass_on(6, 0, -1, 0)
    half = jnp.where(c == 0, 2, -2)
    copy = gather(4, 0, ag.at[jnp.where(c == 0, 2, 6) * X], plane(0, -half))
    copy.start()
    gathers.append(copy)
    for dx in (1, 3, 2):
        arrived(0, dx)
        for ey in (2, -2) if dx == 2 else ():
            pass_on(0, dx, ey, 0)
        for ey in (1, -1):
            pass_on(0, dx, ey, 0)
    for dy in (2, 6):
        for ex in (1, -1):
            pass_on(dy, 0, 0, ex)
    hear(0)
    tell(1)
    for q in range(3, J // 2):
        cycle_product(q)
    cycle_swap = remote(pc.at[1 - c], rc, x_s.at[0], x_r.at[0], sibling)
    cycle_swap.start()
    for dy in (3, 5, 4):
        arrived(dy, 0)
        for ex in X_FAR:
            pass_on(dy, 0, 0, ex)
    hear(1)
    tell(2)
    for dy in (1, 7):
        arrived(dy, 0)

    cycle_swap.wait()
    hear(2)
    cycle_sends = []
    rc[...] = rc[...] + pc[c]
    code, cycle_power = encode(rc[...])
    qc[...] = code.astype(jnp.int16)
    ec[...] = cycle_power
    for k in range(Z - 1):
        zd = target(k)
        slot = lax.rem(z - zd + Z, Z) - 1
        copy = remote(qc.at[zd], zc.at[slot], zc_s.at[k], zc_r.at[slot], place_of(zd))
        copy.start()
        cycle_sends.append(copy)

    for copy in load_g:
        copy.wait()
    swaps, ladder_sends = [], []

    def pick(group, ils):
        for il in ils:
            dy, dx = GROUPS[group][il]
            if dx and dy:
                arrived(dy, dx)
            place(group, il)

    def multiply(group):
        for k in range(CW):
            rhs[group, :, k * TILE : (k + 1) * TILE] = mf[group, k * GC : (k + 1) * GC, :].astype(BF16)
        ladder = lax.dot_general(
            gv[...], rhs[group], (((1,), (1,)), ((), ())), preferred_element_type=F32
        )
        for zd in range(Z):
            for cd in range(2):
                rows = ladder[zd * 32 + cd * 16 : zd * 32 + cd * 16 + 16, :]
                pz[group, cd, zd, :16, :] = rows[:, :TILE]
                pz[group, cd, zd, 16:, :] = jnp.concatenate([rows[:8, TILE:], rows[8:, TILE:]], axis=1)
        swap = remote(pz.at[group, 1 - c], rz.at[group], x_s.at[1 + group], x_r.at[1 + group], sibling)
        swap.start()
        swaps.append(swap)

    def scatter(group):
        swaps[group].wait()
        rz[group] = rz[group] + pz[group, c]
        code, power = encode(rz[group])
        powers = [jnp.broadcast_to(p, (Z, 4, TILE)).astype(jnp.int32) for p in (power, ec[...])]
        qz[group] = jnp.concatenate([code] + powers, axis=1).astype(jnp.int16)
        for k in range(Z - 1):
            zd = target(k)
            slot = lax.rem(z - zd + Z, Z) - 1
            copy = remote(
                qz.at[group, zd], zr.at[group, slot], zl_s.at[group, k], zl_r.at[group, slot], place_of(zd)
            )
            copy.start()
            ladder_sends.append(copy)

    pick(0, range(GI))
    multiply(0)
    pick(1, range(4))
    scatter(0)
    pick(1, range(4, GI))
    multiply(1)
    for copy in gathers:
        copy.wait_send()
    scatter(1)

    cycle = rc[z]
    for dz in range(1, Z):
        remote(qc.at[0], zc.at[dz - 1], zc_s.at[0], zc_r.at[dz - 1], column(-dz)).wait_recv()
    for copy in cycle_sends:
        copy.wait_send()

    lane = lax.broadcasted_iota(jnp.int32, (GI, TILE), 1)
    blocks = []
    for group in range(2):
        total = rz[group, z]
        for dz in (1, 11, 2, 10, 3, 9, 4, 8, 5, 7, 6):
            remote(
                qz.at[group, 0], zr.at[group, dz - 1], zl_s.at[group, 0], zl_r.at[group, dz - 1], column(-dz)
            ).wait_recv()
            received = zr[group, dz - 1].astype(jnp.int32).astype(F32)
            total = total + decode(received[:24, :], received[24:25, :])
            if group == 0:
                cycle = cycle + decode(zc[dz - 1].astype(jnp.int32).astype(F32), received[28:29, :])
        r1[:24, :] = total
        r1[24:, :] = pltpu.roll(total[16:, :], 64, 1)
        flipped = jnp.concatenate(
            [
                jnp.transpose(jnp.concatenate([r1[pl.ds(16 * k + b, 4, stride=4), :] for b in range(4)], axis=0))
                for k in range(2)
            ],
            axis=0,
        )
        pieces = [jnp.zeros((GI, TILE), F32) for _ in range(4)]
        for j in range(J):
            block = jnp.concatenate(
                [flipped[j * GI : (j + 1) * GI, :], jnp.zeros((GI, TILE - 16), F32)], axis=1
            )
            block = pltpu.roll(block, 4 * j, 1)
            for b in range(4):
                low = 4 * (j + b)
                pieces[b] = jnp.where((lane >= low) & (lane < low + 4), block, pieces[b])
        for b in range(4):
            piece = pieces[b] if b == 0 else pltpu.roll(pieces[b], TILE - 4 * b, 1)
            w2[pl.ds(b, GI, stride=4), :] = piece
        w3[group] = w2[...].reshape(GI, 4, TILE)
        for il in sorted(range(GI), key=lambda il: -hops(GROUPS[group][il])):
            dy, dx = GROUPS[group][il]
            if (dy, dx) == (0, 0):
                own = pltpu.make_async_copy(w3.at[group, il], zz.at[t], self_sem)
                own.start()
                own.wait()
                continue
            slot = dy * X + dx
            copy = remote(w3.at[group, il], zz.at[t], a2a_s.at[slot], a2a_r.at[t], plane(dx, dy))
            copy.start()
            blocks.append(copy)
    for copy in ladder_sends:
        copy.wait_send()
    for dx, dy in others:
        src = plane(dx, dy)["tensor"]
        remote(w3.at[0, 0], zz.at[src], a2a_s.at[0], a2a_r.at[src], plane(dx, dy)).wait_recv()
    final = jnp.transpose(zz[...].reshape(PLANE * 4, TILE))
    out[...] = (final[: J * 4, :] + cycle).astype(BF16)
    for copy in blocks:
        copy.wait_send()


def body(amplitudes, pair_mask, tile_mask, cycle_integrals, ladder_integrals):
    w = jnp.transpose(cycle_integrals, (0, 2, 1, 3))
    g = jnp.transpose(ladder_integrals, (0, 2, 3, 1)).reshape(CW, AB, TILE)
    smem = pl.BlockSpec(memory_space=pltpu.SMEM)
    anywhere = pl.BlockSpec(memory_space=pl.ANY)
    dma = pltpu.SemaphoreType.DMA
    out = pl.pallas_call(
        kernel,
        out_shape=jax.ShapeDtypeStruct((J * 4, TILE), BF16),
        in_specs=[smem, smem, anywhere, anywhere, anywhere],
        out_specs=pl.BlockSpec(memory_space=pltpu.VMEM),
        scratch_shapes=[
            pltpu.VMEM((J, WIN, TILE), BF16),
            pltpu.VMEM((WIN, J * TILE), BF16),
            pltpu.VMEM((J, J, TILE, TILE), BF16),
            pltpu.VMEM((AB, CW * TILE), BF16),
            pltpu.VMEM((PLANE, J * CW, TILE), BF16),
            pltpu.VMEM((2, CW * GC, TILE), F32),
            pltpu.VMEM((2, GC, CW * TILE), BF16),
            pltpu.VMEM((2, Z, J * 4, TILE), F32),
            pltpu.VMEM((Z, J * 4, TILE), F32),
            pltpu.VMEM((Z, J * 4, TILE), jnp.int16),
            pltpu.VMEM((Z, 1, TILE), F32),
            pltpu.VMEM((Z - 1, J * 4, TILE), jnp.int16),
            pltpu.VMEM((2, 2, Z, 24, TILE), F32),
            pltpu.VMEM((2, Z, 24, TILE), F32),
            pltpu.VMEM((2, Z, 32, TILE), jnp.int16),
            pltpu.VMEM((2, Z - 1, 32, TILE), jnp.int16),
            pltpu.VMEM((32, TILE), F32),
            pltpu.VMEM((GI * 4, TILE), F32),
            pltpu.VMEM((2, GI, 4, TILE), F32),
            pltpu.VMEM((PLANE, 4, TILE), F32),
            dma((1 + CW,)), dma((J // 2,)), dma((PLANE,)), dma((PLANE,)), dma((3,)), dma((3,)),
            dma((Z - 1,)), dma((Z - 1,)), dma((2, Z - 1)), dma((2, Z - 1)), dma((PLANE,)), dma((PLANE,)),
            dma, pltpu.SemaphoreType.REGULAR((3,)),
        ],
        compiler_params=pltpu.CompilerParams(
            collective_id=0, has_side_effects=True, vmem_limit_bytes=60 * 2**20
        ),
    )(pair_mask, tile_mask.reshape(1, -1), amplitudes[0], w, g)
    return out.reshape(1, J, 4, TILE)


def solution(mesh):
    in_specs = (
        P("tensor", None, None, "contract"),
        P("tensor", None),
        P(),
        P(None, "contract", None, None),
        P(None, "contract", None, "tensor"),
    )
    out_specs = P("tensor", None, "contract", None)
    return jax.shard_map(body, mesh=mesh, in_specs=in_specs, out_specs=out_specs, check_vma=False)
```

```python
import jax
import jax.numpy as jnp
from jax import lax
from jax.experimental import pallas as pl
from jax.experimental.pallas import tpu as pltpu
from jax.sharding import PartitionSpec as P

X, Y, Z = 4, 8, 12
PLANE = X * Y
J, WIN, TILE, CW, AB = 12, 96, 128, 8, 384
MESH = pl.DeviceIdType.MESH
F32, BF16 = jnp.float32, jnp.bfloat16
Y_NEAR = (2, 6, 1, 7)
X_FAR = (2, 1, 3)
GI = 16
STEPS = 32000.0
GC = J * GI
GROUPS = tuple(
    tuple((dy, dx) for dy in rows for dx in (0, 1, 3, 2)) for rows in ((0, 1, 7, 2), (6, 3, 5, 4))
)
Z_FAR = (6, 5, 7, 4, 8, 3, 9, 2, 10, 1, 11)


def hops(slot):
    dy, dx = slot
    return min(dy, Y - dy) + min(dx, X - dx)


def encode(values):
    top = jnp.max(jnp.abs(values), axis=1, keepdims=True)
    power = jnp.ceil(jnp.log2(jnp.maximum(top, 1e-36)))
    return jnp.round(values * jnp.exp2(-power) * STEPS).astype(jnp.int32), power


def decode(code, power):
    return code * (1.0 / STEPS) * jnp.exp2(power)


def kernel(
    pm, tm, a_hbm, w_hbm, g_hbm, out,
    av, am, wv, gv, ag, mf, rhs, pc, rc, qc, ec, zc, pz, rz, qz, zr, r1, w2, w3, zz,
    load_sem, w_sem, ag_s, ag_r, x_s, x_r, zc_s, zc_r, zl_s, zl_r, a2a_s, a2a_r, self_sem, known,
):
    t = lax.axis_index("tensor")
    s = lax.axis_index("contract")
    x, y, z, c = t // Y, t % Y, s // 2, s % 2

    def plane(dx, dy):
        return {"tensor": lax.rem(x + dx + X, X) * Y + lax.rem(y + dy + Y, Y), "contract": s}

    def column(dz):
        return {"tensor": t, "contract": lax.rem(z + dz + Z, Z) * 2 + c}

    def target(k):
        return jnp.where(k >= z, k + 1, k)

    def place_of(zd):
        return {"tensor": t, "contract": zd * 2 + c}

    sibling = {"tensor": t, "contract": z * 2 + 1 - c}

    def remote(src, dst, ss, rs, to):
        return pltpu.make_async_remote_copy(
            src_ref=src, dst_ref=dst, send_sem=ss, recv_sem=rs, device_id=to, device_id_type=MESH
        )

    barrier = pltpu.get_barrier_semaphore()
    others = [(dx, dy) for dx in range(X) for dy in range(Y) if (dx, dy) != (0, 0)]
    line = [plane(0, dy) for dy in Y_NEAR] + [plane(dx, 0) for dx in X_FAR]
    line += [column(1), column(-1), sibling]
    for peer in line:
        pl.semaphore_signal(barrier, inc=1, device_id=peer, device_id_type=MESH)
    load_a = pltpu.make_async_copy(a_hbm, av, load_sem.at[0])
    load_a.start()
    load_w = [
        pltpu.make_async_copy(w_hbm.at[:, 2 * q : 2 * q + 2], wv.at[:, 2 * q : 2 * q + 2], w_sem.at[q])
        for q in range(J // 2)
    ]
    for copy in load_w:
        copy.start()
    load_g = [
        pltpu.make_async_copy(g_hbm.at[k], gv.at[:, k * TILE : (k + 1) * TILE], load_sem.at[1 + k])
        for k in range(CW)
    ]
    for copy in load_g:
        copy.start()

    load_a.wait()
    kept = tm[0, s].astype(F32)
    for j in range(J):
        m = pm[0, j].astype(F32)
        ag[0, j * CW : (j + 1) * CW, :] = (av[j, :CW, :].astype(F32) * (m * kept)).astype(BF16)
    pl.semaphore_wait(barrier, len(line))

    def tell(level):
        for dz in (2**level, -(2**level)):
            pl.semaphore_signal(known.at[level], inc=1, device_id=column(dz), device_id_type=MESH)

    def hear(level):
        pl.semaphore_wait(known.at[level], 2)

    tell(0)

    def gather(dy, dx, src, to):
        slot = dy * X + dx
        return remote(src, ag.at[slot], ag_s.at[slot], ag_r.at[slot], to)

    gathers = []
    for dy in Y_NEAR:
        gathers.append(gather(dy, 0, ag.at[0], plane(0, -dy)))
    for dx in X_FAR:
        gathers.append(gather(0, dx, ag.at[0], plane(-dx, 0)))
    for copy in gathers:
        copy.start()

    def place(group, il):
        dy, dx = GROUPS[group][il]
        block = ag[dy * X + dx].astype(F32)
        for j in range(J):
            mf[group, pl.ds(j * GI + il, CW, stride=GC), :] = block[j * CW : (j + 1) * CW, :]

    for j in range(J):
        m = pm[0, j].astype(F32)
        am[:, j * TILE : (j + 1) * TILE] = (av[j].astype(F32) * m).astype(BF16)

    def cycle_product(q):
        load_w[q].wait()
        right = jnp.concatenate(
            [wv[:, 2 * q + h].reshape(J * TILE, TILE) for h in range(2)], axis=1
        )
        product = jnp.dot(am[...], right, preferred_element_type=F32)
        for zd in range(Z):
            for cd in range(2):
                rows = product[zd * 8 + cd * 4 : zd * 8 + cd * 4 + 4, :]
                pc[cd, zd, 8 * q : 8 * q + 8, :] = jnp.concatenate([rows[:, :TILE], rows[:, TILE:]], axis=0)

    def arrived(dy, dx):
        gather(dy, dx, ag.at[0], sibling).wait_recv()

    def pass_on(dy, dx, ey, ex):
        copy = gather((dy + ey) % Y, (dx + ex) % X, ag.at[dy * X + dx], plane(-ex, -ey))
        copy.start()
        gathers.append(copy)

    for q in range(3):
        cycle_product(q)
    hear(0)
    tell(1)
    arrived(2, 0)
    pass_on(2, 0, 1, 0)
    arrived(6, 0)
    pass_on(6, 0, -1, 0)
    half = jnp.where(c == 0, 2, -2)
    copy = gather(4, 0, ag.at[jnp.where(c == 0, 2, 6) * X], plane(0, -half))
    copy.start()
    gathers.append(copy)
    for dx in (1, 3, 2):
        arrived(0, dx)
        for ey in (2, -2) if dx == 2 else ():
            pass_on(0, dx, ey, 0)
        for ey in (1, -1):
            pass_on(0, dx, ey, 0)
    for dy in (2, 6):
        for ex in (1, -1):
            pass_on(dy, 0, 0, ex)
    hear(1)
    tell(2)
    for q in range(3, J // 2):
        cycle_product(q)
    cycle_swap = remote(pc.at[1 - c], rc, x_s.at[0], x_r.at[0], sibling)
    cycle_swap.start()
    for dy in (3, 5, 4):
        arrived(dy, 0)
        for ex in X_FAR:
            pass_on(dy, 0, 0, ex)
    for dy in (1, 7):
        arrived(dy, 0)

    cycle_swap.wait()
    hear(2)
    cycle_sends = []
    rc[...] = rc[...] + pc[c]
    code, cycle_power = encode(rc[...])
    qc[...] = code.astype(jnp.int16)
    ec[...] = cycle_power
    for k in range(Z - 1):
        zd = target(k)
        slot = lax.rem(z - zd + Z, Z) - 1
        copy = remote(qc.at[zd], zc.at[slot], zc_s.at[k], zc_r.at[slot], place_of(zd))
        copy.start()
        cycle_sends.append(copy)

    for copy in load_g:
        copy.wait()
    swaps, ladder_sends = [], []

    def pick(group, ils):
        for il in ils:
            dy, dx = GROUPS[group][il]
            if dx and dy:
                arrived(dy, dx)
            place(group, il)

    def multiply(group):
        for k in range(CW):
            rhs[group, :, k * TILE : (k + 1) * TILE] = mf[group, k * GC : (k + 1) * GC, :].astype(BF16)
        ladder = lax.dot_general(
            gv[...], rhs[group], (((1,), (1,)), ((), ())), preferred_element_type=F32
        )
        for zd in range(Z):
            for cd in range(2):
                rows = ladder[zd * 32 + cd * 16 : zd * 32 + cd * 16 + 16, :]
                pz[group, cd, zd, :16, :] = rows[:, :TILE]
                pz[group, cd, zd, 16:, :] = jnp.concatenate([rows[:8, TILE:], rows[8:, TILE:]], axis=1)
        swap = remote(pz.at[group, 1 - c], rz.at[group], x_s.at[1 + group], x_r.at[1 + group], sibling)
        swap.start()
        swaps.append(swap)

    def scatter(group):
        swaps[group].wait()
        rz[group] = rz[group] + pz[group, c]
        code, power = encode(rz[group])
        powers = [jnp.broadcast_to(p, (Z, 4, TILE)).astype(jnp.int32) for p in (power, ec[...])]
        qz[group] = jnp.concatenate([code] + powers, axis=1).astype(jnp.int16)
        for k in range(Z - 1):
            zd = target(k)
            slot = lax.rem(z - zd + Z, Z) - 1
            copy = remote(
                qz.at[group, zd], zr.at[group, slot], zl_s.at[group, k], zl_r.at[group, slot], place_of(zd)
            )
            copy.start()
            ladder_sends.append(copy)

    pick(0, range(GI))
    multiply(0)
    pick(1, range(4))
    scatter(0)
    pick(1, range(4, GI))
    multiply(1)
    for copy in gathers:
        copy.wait_send()
    scatter(1)

    cycle = rc[z]
    for dz in range(1, Z):
        remote(qc.at[0], zc.at[dz - 1], zc_s.at[0], zc_r.at[dz - 1], column(-dz)).wait_recv()
    for copy in cycle_sends:
        copy.wait_send()

    lane = lax.broadcasted_iota(jnp.int32, (GI, TILE), 1)
    blocks = []
    for group in range(2):
        total = rz[group, z]
        for dz in (1, 11, 2, 10, 3, 9, 4, 8, 5, 7, 6):
            remote(
                qz.at[group, 0], zr.at[group, dz - 1], zl_s.at[group, 0], zl_r.at[group, dz - 1], column(-dz)
            ).wait_recv()
            received = zr[group, dz - 1].astype(jnp.int32).astype(F32)
            total = total + decode(received[:24, :], received[24:25, :])
            if group == 0:
                cycle = cycle + decode(zc[dz - 1].astype(jnp.int32).astype(F32), received[28:29, :])
        r1[:24, :] = total
        r1[24:, :] = pltpu.roll(total[16:, :], 64, 1)
        flipped = jnp.concatenate(
            [
                jnp.transpose(jnp.concatenate([r1[pl.ds(16 * k + b, 4, stride=4), :] for b in range(4)], axis=0))
                for k in range(2)
            ],
            axis=0,
        )
        pieces = [jnp.zeros((GI, TILE), F32) for _ in range(4)]
        for j in range(J):
            block = jnp.concatenate(
                [flipped[j * GI : (j + 1) * GI, :], jnp.zeros((GI, TILE - 16), F32)], axis=1
            )
            block = pltpu.roll(block, 4 * j, 1)
            for b in range(4):
                low = 4 * (j + b)
                pieces[b] = jnp.where((lane >= low) & (lane < low + 4), block, pieces[b])
        for b in range(4):
            piece = pieces[b] if b == 0 else pltpu.roll(pieces[b], TILE - 4 * b, 1)
            w2[pl.ds(b, GI, stride=4), :] = piece
        w3[group] = w2[...].reshape(GI, 4, TILE)
        for il in sorted(range(GI), key=lambda il: -hops(GROUPS[group][il])):
            dy, dx = GROUPS[group][il]
            if (dy, dx) == (0, 0):
                own = pltpu.make_async_copy(w3.at[group, il], zz.at[t], self_sem)
                own.start()
                own.wait()
                continue
            slot = dy * X + dx
            copy = remote(w3.at[group, il], zz.at[t], a2a_s.at[slot], a2a_r.at[t], plane(dx, dy))
            copy.start()
            blocks.append(copy)
    for copy in ladder_sends:
        copy.wait_send()
    for dx, dy in others:
        src = plane(dx, dy)["tensor"]
        remote(w3.at[0, 0], zz.at[src], a2a_s.at[0], a2a_r.at[src], plane(dx, dy)).wait_recv()
    final = jnp.transpose(zz[...].reshape(PLANE * 4, TILE))
    out[...] = (final[: J * 4, :] + cycle).astype(BF16)
    for copy in blocks:
        copy.wait_send()


def body(amplitudes, pair_mask, tile_mask, cycle_integrals, ladder_integrals):
    w = jnp.transpose(cycle_integrals, (0, 2, 1, 3))
    g = jnp.transpose(ladder_integrals, (0, 2, 3, 1)).reshape(CW, AB, TILE)
    smem = pl.BlockSpec(memory_space=pltpu.SMEM)
    anywhere = pl.BlockSpec(memory_space=pl.ANY)
    dma = pltpu.SemaphoreType.DMA
    out = pl.pallas_call(
        kernel,
        out_shape=jax.ShapeDtypeStruct((J * 4, TILE), BF16),
        in_specs=[smem, smem, anywhere, anywhere, anywhere],
        out_specs=pl.BlockSpec(memory_space=pltpu.VMEM),
        scratch_shapes=[
            pltpu.VMEM((J, WIN, TILE), BF16),
            pltpu.VMEM((WIN, J * TILE), BF16),
            pltpu.VMEM((J, J, TILE, TILE), BF16),
            pltpu.VMEM((AB, CW * TILE), BF16),
            pltpu.VMEM((PLANE, J * CW, TILE), BF16),
            pltpu.VMEM((2, CW * GC, TILE), F32),
            pltpu.VMEM((2, GC, CW * TILE), BF16),
            pltpu.VMEM((2, Z, J * 4, TILE), F32),
            pltpu.VMEM((Z, J * 4, TILE), F32),
            pltpu.VMEM((Z, J * 4, TILE), jnp.int16),
            pltpu.VMEM((Z, 1, TILE), F32),
            pltpu.VMEM((Z - 1, J * 4, TILE), jnp.int16),
            pltpu.VMEM((2, 2, Z, 24, TILE), F32),
            pltpu.VMEM((2, Z, 24, TILE), F32),
            pltpu.VMEM((2, Z, 32, TILE), jnp.int16),
            pltpu.VMEM((2, Z - 1, 32, TILE), jnp.int16),
            pltpu.VMEM((32, TILE), F32),
            pltpu.VMEM((GI * 4, TILE), F32),
            pltpu.VMEM((2, GI, 4, TILE), F32),
            pltpu.VMEM((PLANE, 4, TILE), F32),
            dma((1 + CW,)), dma((J // 2,)), dma((PLANE,)), dma((PLANE,)), dma((3,)), dma((3,)),
            dma((Z - 1,)), dma((Z - 1,)), dma((2, Z - 1)), dma((2, Z - 1)), dma((PLANE,)), dma((PLANE,)),
            dma, pltpu.SemaphoreType.REGULAR((3,)),
        ],
        compiler_params=pltpu.CompilerParams(
            collective_id=0, has_side_effects=True, vmem_limit_bytes=60 * 2**20
        ),
    )(pair_mask, tile_mask.reshape(1, -1), amplitudes[0], w, g)
    return out.reshape(1, J, 4, TILE)


def solution(mesh):
    in_specs = (
        P("tensor", None, None, "contract"),
        P("tensor", None),
        P(),
        P(None, "contract", None, None),
        P(None, "contract", None, "tensor"),
    )
    out_specs = P("tensor", None, "contract", None)
    return jax.shard_map(body, mesh=mesh, in_specs=in_specs, out_specs=out_specs, check_vma=False)
```

```python
import jax
import jax.numpy as jnp
from jax import lax
from jax.experimental import pallas as pl
from jax.experimental.pallas import tpu as pltpu
from jax.sharding import PartitionSpec as P

X, Y, Z = 4, 8, 12
PLANE = X * Y
J, WIN, TILE, CW, AB = 12, 96, 128, 8, 384
MESH = pl.DeviceIdType.MESH
F32, BF16 = jnp.float32, jnp.bfloat16
Y_NEAR = (2, 6, 1, 7)
X_FAR = (2, 1, 3)
GN = 4
GI = 8
STEPS = 32000.0
GC = J * GI
GROUPS = tuple(
    tuple((dy, dx) for dy in rows for dx in (0, 1, 3, 2)) for rows in ((0, 1), (7, 2), (6, 3), (5, 4))
)
Z_FAR = (6, 5, 7, 4, 8, 3, 9, 2, 10, 1, 11)


def hops(slot):
    dy, dx = slot
    return min(dy, Y - dy) + min(dx, X - dx)


def encode(values, shifts=()):
    top = jnp.max(jnp.abs(values), axis=1, keepdims=True)
    for shift in shifts:
        top = jnp.maximum(top, pltpu.roll(top, shift, 2))
    power = jnp.ceil(jnp.log2(jnp.maximum(top, 1e-36)))
    return jnp.round(values * jnp.exp2(-power) * STEPS).astype(jnp.int32), power


def decode(code, power):
    return code * (1.0 / STEPS) * jnp.exp2(power)


def kernel(
    pm, tm, a_hbm, w_hbm, g_hbm, out,
    av, am, wv, gv, ag, mf, rhs, pc, rc, qc, zc, pz, rz, qz, zr, r1, w2, w3, zz,
    load_sem, w_sem, ag_s, ag_r, x_s, x_r, zc_s, zc_r, zl_s, zl_r, a2a_s, a2a_r, self_sem, known,
):
    t = lax.axis_index("tensor")
    s = lax.axis_index("contract")
    x, y, z, c = t // Y, t % Y, s // 2, s % 2

    def plane(dx, dy):
        return {"tensor": lax.rem(x + dx + X, X) * Y + lax.rem(y + dy + Y, Y), "contract": s}

    def column(dz):
        return {"tensor": t, "contract": lax.rem(z + dz + Z, Z) * 2 + c}

    def target(k):
        return jnp.where(k >= z, k + 1, k)

    def place_of(zd):
        return {"tensor": t, "contract": zd * 2 + c}

    sibling = {"tensor": t, "contract": z * 2 + 1 - c}

    def remote(src, dst, ss, rs, to):
        return pltpu.make_async_remote_copy(
            src_ref=src, dst_ref=dst, send_sem=ss, recv_sem=rs, device_id=to, device_id_type=MESH
        )

    barrier = pltpu.get_barrier_semaphore()
    others = [(dx, dy) for dx in range(X) for dy in range(Y) if (dx, dy) != (0, 0)]
    line = [plane(0, dy) for dy in Y_NEAR] + [plane(dx, 0) for dx in X_FAR]
    line += [column(1), column(-1), sibling]
    for peer in line:
        pl.semaphore_signal(barrier, inc=1, device_id=peer, device_id_type=MESH)
    load_a = pltpu.make_async_copy(a_hbm, av, load_sem.at[0])
    load_a.start()
    load_w = [
        pltpu.make_async_copy(w_hbm.at[:, 2 * q : 2 * q + 2], wv.at[:, 2 * q : 2 * q + 2], w_sem.at[q])
        for q in range(J // 2)
    ]
    for copy in load_w:
        copy.start()
    load_g = [
        pltpu.make_async_copy(g_hbm.at[k], gv.at[:, k * TILE : (k + 1) * TILE], load_sem.at[1 + k])
        for k in range(CW)
    ]
    for copy in load_g:
        copy.start()

    load_a.wait()
    kept = tm[0, s].astype(F32)
    for j in range(J):
        m = pm[0, j].astype(F32)
        ag[0, j * CW : (j + 1) * CW, :] = (av[j, :CW, :].astype(F32) * (m * kept)).astype(BF16)
    pl.semaphore_wait(barrier, len(line))

    def tell(level):
        for dz in (2**level, -(2**level)):
            pl.semaphore_signal(known.at[level], inc=1, device_id=column(dz), device_id_type=MESH)

    def hear(level):
        pl.semaphore_wait(known.at[level], 2)

    tell(0)

    def gather(dy, dx, src, to):
        slot = dy * X + dx
        return remote(src, ag.at[slot], ag_s.at[slot], ag_r.at[slot], to)

    gathers = []
    for dy in Y_NEAR:
        gathers.append(gather(dy, 0, ag.at[0], plane(0, -dy)))
    for dx in X_FAR:
        gathers.append(gather(0, dx, ag.at[0], plane(-dx, 0)))
    for copy in gathers:
        copy.start()

    def place(group, il):
        dy, dx = GROUPS[group][il]
        block = ag[dy * X + dx].astype(F32)
        for j in range(J):
            mf[group, pl.ds(j * GI + il, CW, stride=GC), :] = block[j * CW : (j + 1) * CW, :]

    for j in range(J):
        m = pm[0, j].astype(F32)
        am[:, j * TILE : (j + 1) * TILE] = (av[j].astype(F32) * m).astype(BF16)

    def cycle_product(q):
        load_w[q].wait()
        right = jnp.concatenate(
            [wv[:, 2 * q + h].reshape(J * TILE, TILE) for h in range(2)], axis=1
        )
        product = jnp.dot(am[...], right, preferred_element_type=F32)
        for zd in range(Z):
            for cd in range(2):
                rows = product[zd * 8 + cd * 4 : zd * 8 + cd * 4 + 4, :]
                pc[cd, zd, 8 * q : 8 * q + 8, :] = jnp.concatenate([rows[:, :TILE], rows[:, TILE:]], axis=0)

    def arrived(dy, dx):
        gather(dy, dx, ag.at[0], sibling).wait_recv()

    def pass_on(dy, dx, ey, ex):
        copy = gather((dy + ey) % Y, (dx + ex) % X, ag.at[dy * X + dx], plane(-ex, -ey))
        copy.start()
        gathers.append(copy)

    for q in range(3):
        cycle_product(q)
    hear(0)
    tell(1)
    arrived(2, 0)
    pass_on(2, 0, 1, 0)
    arrived(6, 0)
    pass_on(6, 0, -1, 0)
    half = jnp.where(c == 0, 2, -2)
    copy = gather(4, 0, ag.at[jnp.where(c == 0, 2, 6) * X], plane(0, -half))
    copy.start()
    gathers.append(copy)
    for dx in (1, 3, 2):
        arrived(0, dx)
        for ey in (2, -2) if dx == 2 else ():
            pass_on(0, dx, ey, 0)
        for ey in (1, -1):
            pass_on(0, dx, ey, 0)
    for dy in (2, 6):
        for ex in (1, -1):
            pass_on(dy, 0, 0, ex)
    hear(1)
    tell(2)
    for q in range(3, J // 2):
        cycle_product(q)
    cycle_swap = remote(pc.at[1 - c], rc, x_s.at[0], x_r.at[0], sibling)
    cycle_swap.start()
    for dy in (3, 5, 4):
        arrived(dy, 0)
        for ex in X_FAR:
            pass_on(dy, 0, 0, ex)
    for dy in (1, 7):
        arrived(dy, 0)

    cycle_swap.wait()
    hear(2)
    cycle_sends = []
    rc[...] = rc[...] + pc[c]
    code, power = encode(rc[...])
    power = jnp.broadcast_to(power, (Z, 16, TILE)).astype(jnp.int32)
    qc[...] = jnp.concatenate([code, power], axis=1).astype(jnp.int16)
    for k in range(Z - 1):
        zd = target(k)
        slot = lax.rem(z - zd + Z, Z) - 1
        copy = remote(qc.at[zd], zc.at[slot], zc_s.at[k], zc_r.at[slot], place_of(zd))
        copy.start()
        cycle_sends.append(copy)

    for copy in load_g:
        copy.wait()
    swaps, ladder_sends = [], []

    def pick(group, ils):
        for il in ils:
            dy, dx = GROUPS[group][il]
            if dx and dy:
                arrived(dy, dx)
            place(group, il)

    def multiply(group):
        for k in range(CW):
            rhs[group, :, k * TILE : (k + 1) * TILE] = mf[group, k * GC : (k + 1) * GC, :].astype(BF16)
        ladder = lax.dot_general(
            gv[...], rhs[group], (((1,), (1,)), ((), ())), preferred_element_type=F32
        )
        for zd in range(Z):
            for cd in range(2):
                rows = ladder[zd * 32 + cd * 16 : zd * 32 + cd * 16 + 16, :]
                pz[group, cd, zd] = jnp.concatenate([rows, jnp.zeros((16, TILE - GC), F32)], axis=1)
        swap = remote(pz.at[group, 1 - c], rz.at[group], x_s.at[1 + group], x_r.at[1 + group], sibling)
        swap.start()
        swaps.append(swap)

    def scatter(group):
        swaps[group].wait()
        rz[group] = rz[group] + pz[group, c]
        code, power = encode(rz[group], (32, 64))
        column_of = lax.broadcasted_iota(jnp.int32, (Z, 16, TILE), 2)
        power = jnp.broadcast_to(power, (Z, 16, TILE)).astype(jnp.int32)
        qz[group] = jnp.where(column_of >= GC, power, code).astype(jnp.int16)
        for k in range(Z - 1):
            zd = target(k)
            slot = lax.rem(z - zd + Z, Z) - 1
            copy = remote(
                qz.at[group, zd], zr.at[group, slot], zl_s.at[group, k], zl_r.at[group, slot], place_of(zd)
            )
            copy.start()
            ladder_sends.append(copy)

    for group in range(GN):
        pick(group, range(GI))
        if group:
            scatter(group - 1)
        multiply(group)
    for copy in gathers:
        copy.wait_send()
    scatter(GN - 1)

    cycle = rc[z]
    for dz in range(1, Z):
        remote(qc.at[0], zc.at[dz - 1], zc_s.at[0], zc_r.at[dz - 1], column(-dz)).wait_recv()
        received = zc[dz - 1].astype(jnp.int32).astype(F32)
        cycle = cycle + decode(received[: J * 4, :], received[J * 4 : J * 4 + 1, :])
    for copy in cycle_sends:
        copy.wait_send()

    lane = lax.broadcasted_iota(jnp.int32, (GI, TILE), 1)
    lanes = lax.broadcasted_iota(jnp.int32, (16, TILE), 1)
    blocks = []
    for group in range(GN):
        total = rz[group, z]
        for dz in (1, 11, 2, 10, 3, 9, 4, 8, 5, 7, 6):
            remote(
                qz.at[group, 0], zr.at[group, dz - 1], zl_s.at[group, 0], zl_r.at[group, dz - 1], column(-dz)
            ).wait_recv()
            received = zr[group, dz - 1].astype(jnp.int32).astype(F32)
            power = jnp.where(lanes >= GC, received, 0.0)
            power = power + pltpu.roll(power, 64, 1)
            power = power + pltpu.roll(power, 32, 1)
            total = total + decode(received, power)
        r1[...] = total
        flipped = jnp.transpose(jnp.concatenate([r1[pl.ds(b, 4, stride=4), :] for b in range(4)], axis=0))
        pieces = [jnp.zeros((GI, TILE), F32) for _ in range(4)]
        for j in range(J):
            block = jnp.concatenate(
                [flipped[j * GI : (j + 1) * GI, :], jnp.zeros((GI, TILE - 16), F32)], axis=1
            )
            block = pltpu.roll(block, 4 * j, 1)
            for b in range(4):
                low = 4 * (j + b)
                pieces[b] = jnp.where((lane >= low) & (lane < low + 4), block, pieces[b])
        for b in range(4):
            piece = pieces[b] if b == 0 else pltpu.roll(pieces[b], TILE - 4 * b, 1)
            w2[pl.ds(b, GI, stride=4), :] = piece
        w3[group] = w2[...].reshape(GI, 4, TILE)
        for il in sorted(range(GI), key=lambda il: -hops(GROUPS[group][il])):
            dy, dx = GROUPS[group][il]
            if (dy, dx) == (0, 0):
                own = pltpu.make_async_copy(w3.at[group, il], zz.at[t], self_sem)
                own.start()
                own.wait()
                continue
            slot = dy * X + dx
            copy = remote(w3.at[group, il], zz.at[t], a2a_s.at[slot], a2a_r.at[t], plane(dx, dy))
            copy.start()
            blocks.append(copy)
    for copy in ladder_sends:
        copy.wait_send()
    for dx, dy in others:
        src = plane(dx, dy)["tensor"]
        remote(w3.at[0, 0], zz.at[src], a2a_s.at[0], a2a_r.at[src], plane(dx, dy)).wait_recv()
    final = jnp.transpose(zz[...].reshape(PLANE * 4, TILE))
    out[...] = (final[: J * 4, :] + cycle).astype(BF16)
    for copy in blocks:
        copy.wait_send()


def body(amplitudes, pair_mask, tile_mask, cycle_integrals, ladder_integrals):
    w = jnp.transpose(cycle_integrals, (0, 2, 1, 3))
    g = jnp.transpose(ladder_integrals, (0, 2, 3, 1)).reshape(CW, AB, TILE)
    smem = pl.BlockSpec(memory_space=pltpu.SMEM)
    anywhere = pl.BlockSpec(memory_space=pl.ANY)
    dma = pltpu.SemaphoreType.DMA
    out = pl.pallas_call(
        kernel,
        out_shape=jax.ShapeDtypeStruct((J * 4, TILE), BF16),
        in_specs=[smem, smem, anywhere, anywhere, anywhere],
        out_specs=pl.BlockSpec(memory_space=pltpu.VMEM),
        scratch_shapes=[
            pltpu.VMEM((J, WIN, TILE), BF16),
            pltpu.VMEM((WIN, J * TILE), BF16),
            pltpu.VMEM((J, J, TILE, TILE), BF16),
            pltpu.VMEM((AB, CW * TILE), BF16),
            pltpu.VMEM((PLANE, J * CW, TILE), BF16),
            pltpu.VMEM((GN, CW * GC, TILE), F32),
            pltpu.VMEM((GN, GC, CW * TILE), BF16),
            pltpu.VMEM((2, Z, J * 4, TILE), F32),
            pltpu.VMEM((Z, J * 4, TILE), F32),
            pltpu.VMEM((Z, J * 4 + 16, TILE), jnp.int16),
            pltpu.VMEM((Z - 1, J * 4 + 16, TILE), jnp.int16),
            pltpu.VMEM((GN, 2, Z, 16, TILE), F32),
            pltpu.VMEM((GN, Z, 16, TILE), F32),
            pltpu.VMEM((GN, Z, 16, TILE), jnp.int16),
            pltpu.VMEM((GN, Z - 1, 16, TILE), jnp.int16),
            pltpu.VMEM((16, TILE), F32),
            pltpu.VMEM((GI * 4, TILE), F32),
            pltpu.VMEM((GN, GI, 4, TILE), F32),
            pltpu.VMEM((PLANE, 4, TILE), F32),
            dma((1 + CW,)), dma((J // 2,)), dma((PLANE,)), dma((PLANE,)), dma((1 + GN,)), dma((1 + GN,)),
            dma((Z - 1,)), dma((Z - 1,)), dma((GN, Z - 1)), dma((GN, Z - 1)), dma((PLANE,)), dma((PLANE,)),
            dma, pltpu.SemaphoreType.REGULAR((3,)),
        ],
        compiler_params=pltpu.CompilerParams(
            collective_id=0, has_side_effects=True, vmem_limit_bytes=60 * 2**20
        ),
    )(pair_mask, tile_mask.reshape(1, -1), amplitudes[0], w, g)
    return out.reshape(1, J, 4, TILE)


def solution(mesh):
    in_specs = (
        P("tensor", None, None, "contract"),
        P("tensor", None),
        P(),
        P(None, "contract", None, None),
        P(None, "contract", None, "tensor"),
    )
    out_specs = P("tensor", None, "contract", None)
    return jax.shard_map(body, mesh=mesh, in_specs=in_specs, out_specs=out_specs, check_vma=False)
```

```python
import jax
import jax.numpy as jnp
from jax import lax
from jax.experimental import pallas as pl
from jax.experimental.pallas import tpu as pltpu
from jax.sharding import PartitionSpec as P

X, Y, Z = 4, 8, 12
PLANE = X * Y
J, WIN, TILE, CW, AB = 12, 96, 128, 8, 384
MESH = pl.DeviceIdType.MESH
F32, BF16 = jnp.float32, jnp.bfloat16
Y_NEAR = (2, 6, 1, 7)
X_FAR = (2, 1, 3)
GI = 16
STEPS = 32000.0
GC = J * GI
GROUPS = tuple(
    tuple((dy, dx) for dy in rows for dx in (0, 1, 3, 2)) for rows in ((0, 1, 7, 2), (6, 3, 5, 4))
)
Z_FAR = (6, 5, 7, 4, 8, 3, 9, 2, 10, 1, 11)


def hops(slot):
    dy, dx = slot
    return min(dy, Y - dy) + min(dx, X - dx)


def encode(values):
    top = jnp.max(jnp.abs(values), axis=1, keepdims=True)
    power = jnp.ceil(jnp.log2(jnp.maximum(top, 1e-36)))
    return jnp.round(values * jnp.exp2(-power) * STEPS).astype(jnp.int32), power


def decode(code, power):
    return code * (1.0 / STEPS) * jnp.exp2(power)


def kernel(
    pm, tm, a_hbm, w_hbm, g_hbm, out,
    av, am, wv, gv, ag, mf, rhs, pc, rc, qc, ec, zc, pz, rz, qz, zr, r1, w2, w3, zz,
    load_sem, w_sem, ag_s, ag_r, x_s, x_r, zc_s, zc_r, zl_s, zl_r, a2a_s, a2a_r, self_sem, known,
):
    t = lax.axis_index("tensor")
    s = lax.axis_index("contract")
    x, y, z, c = t // Y, t % Y, s // 2, s % 2

    def plane(dx, dy):
        return {"tensor": lax.rem(x + dx + X, X) * Y + lax.rem(y + dy + Y, Y), "contract": s}

    def column(dz):
        return {"tensor": t, "contract": lax.rem(z + dz + Z, Z) * 2 + c}

    def target(k):
        return jnp.where(k >= z, k + 1, k)

    def place_of(zd):
        return {"tensor": t, "contract": zd * 2 + c}

    sibling = {"tensor": t, "contract": z * 2 + 1 - c}

    def remote(src, dst, ss, rs, to):
        return pltpu.make_async_remote_copy(
            src_ref=src, dst_ref=dst, send_sem=ss, recv_sem=rs, device_id=to, device_id_type=MESH
        )

    barrier = pltpu.get_barrier_semaphore()
    others = [(dx, dy) for dx in range(X) for dy in range(Y) if (dx, dy) != (0, 0)]
    line = [plane(0, dy) for dy in Y_NEAR] + [plane(dx, 0) for dx in X_FAR]
    line += [column(1), column(-1), sibling]
    for peer in line:
        pl.semaphore_signal(barrier, inc=1, device_id=peer, device_id_type=MESH)
    load_a = pltpu.make_async_copy(a_hbm, av, load_sem.at[0])
    load_a.start()
    load_w = [
        pltpu.make_async_copy(w_hbm.at[:, 2 * q : 2 * q + 2], wv.at[:, 2 * q : 2 * q + 2], w_sem.at[q])
        for q in range(J // 2)
    ]
    for copy in load_w:
        copy.start()
    load_g = [
        pltpu.make_async_copy(g_hbm.at[k], gv.at[:, k * TILE : (k + 1) * TILE], load_sem.at[1 + k])
        for k in range(CW)
    ]
    for copy in load_g:
        copy.start()

    load_a.wait()
    kept = tm[0, s].astype(F32)
    for j in range(J):
        m = pm[0, j].astype(F32)
        ag[0, j * CW : (j + 1) * CW, :] = (av[j, :CW, :].astype(F32) * (m * kept)).astype(BF16)
    pl.semaphore_wait(barrier, len(line))

    def tell(level):
        for dz in (2**level, -(2**level)):
            pl.semaphore_signal(known.at[level], inc=1, device_id=column(dz), device_id_type=MESH)

    def hear(level):
        pl.semaphore_wait(known.at[level], 2)

    tell(0)

    def gather(dy, dx, src, to):
        slot = dy * X + dx
        return remote(src, ag.at[slot], ag_s.at[slot], ag_r.at[slot], to)

    gathers = []
    for dy, dx in ((2, 0), (6, 0), (0, 2), (0, 1), (0, 3), (1, 0), (7, 0)):
        gathers.append(gather(dy, dx, ag.at[0], plane(-dx, -dy)))
    for copy in gathers:
        copy.start()

    def place(group, il):
        dy, dx = GROUPS[group][il]
        block = ag[dy * X + dx].astype(F32)
        for j in range(J):
            mf[group, pl.ds(j * GI + il, CW, stride=GC), :] = block[j * CW : (j + 1) * CW, :]

    for j in range(J):
        m = pm[0, j].astype(F32)
        am[:, j * TILE : (j + 1) * TILE] = (av[j].astype(F32) * m).astype(BF16)

    def cycle_product(q):
        load_w[q].wait()
        right = jnp.concatenate(
            [wv[:, 2 * q + h].reshape(J * TILE, TILE) for h in range(2)], axis=1
        )
        product = jnp.dot(am[...], right, preferred_element_type=F32)
        for zd in range(Z):
            for cd in range(2):
                rows = product[zd * 8 + cd * 4 : zd * 8 + cd * 4 + 4, :]
                pc[cd, zd, 8 * q : 8 * q + 8, :] = jnp.concatenate([rows[:, :TILE], rows[:, TILE:]], axis=0)

    def arrived(dy, dx):
        gather(dy, dx, ag.at[0], sibling).wait_recv()

    def pass_on(dy, dx, ey, ex):
        copy = gather((dy + ey) % Y, (dx + ex) % X, ag.at[dy * X + dx], plane(-ex, -ey))
        copy.start()
        gathers.append(copy)

    for q in range(3):
        cycle_product(q)
    hear(0)
    tell(1)
    arrived(2, 0)
    pass_on(2, 0, 1, 0)
    arrived(6, 0)
    pass_on(6, 0, -1, 0)
    half = jnp.where(c == 0, 2, -2)
    copy = gather(4, 0, ag.at[jnp.where(c == 0, 2, 6) * X], plane(0, -half))
    copy.start()
    gathers.append(copy)
    for dy in (2, 6):
        for ex in (1, -1):
            pass_on(dy, 0, 0, ex)
    for dx in (1, 3, 2):
        arrived(0, dx)
        for ey in (2, -2) if dx == 2 else ():
            pass_on(0, dx, ey, 0)
        for ey in (1, -1):
            pass_on(0, dx, ey, 0)
    hear(1)
    tell(2)
    for q in range(3, J // 2):
        cycle_product(q)
    cycle_swap = remote(pc.at[1 - c], rc, x_s.at[0], x_r.at[0], sibling)
    cycle_swap.start()
    for dy in (3, 5, 4):
        arrived(dy, 0)
        for ex in X_FAR:
            pass_on(dy, 0, 0, ex)
    for dy in (1, 7):
        arrived(dy, 0)

    cycle_swap.wait()
    hear(2)
    cycle_sends = []
    rc[...] = rc[...] + pc[c]
    code, cycle_power = encode(rc[...])
    qc[...] = code.astype(jnp.int16)
    ec[...] = cycle_power
    for k in range(Z - 1):
        zd = target(k)
        slot = lax.rem(z - zd + Z, Z) - 1
        copy = remote(qc.at[zd], zc.at[slot], zc_s.at[k], zc_r.at[slot], place_of(zd))
        copy.start()
        cycle_sends.append(copy)

    for copy in load_g:
        copy.wait()
    swaps, ladder_sends = [], []

    def pick(group, ils):
        for il in ils:
            dy, dx = GROUPS[group][il]
            if dx and dy:
                arrived(dy, dx)
            place(group, il)

    def multiply(group):
        for k in range(CW):
            rhs[group, :, k * TILE : (k + 1) * TILE] = mf[group, k * GC : (k + 1) * GC, :].astype(BF16)
        ladder = lax.dot_general(
            gv[...], rhs[group], (((1,), (1,)), ((), ())), preferred_element_type=F32
        )
        for zd in range(Z):
            for cd in range(2):
                rows = ladder[zd * 32 + cd * 16 : zd * 32 + cd * 16 + 16, :]
                pz[group, cd, zd, :16, :] = rows[:, :TILE]
                pz[group, cd, zd, 16:, :] = jnp.concatenate([rows[:8, TILE:], rows[8:, TILE:]], axis=1)
        swap = remote(pz.at[group, 1 - c], rz.at[group], x_s.at[1 + group], x_r.at[1 + group], sibling)
        swap.start()
        swaps.append(swap)

    def scatter(group):
        swaps[group].wait()
        rz[group] = rz[group] + pz[group, c]
        code, power = encode(rz[group])
        powers = [jnp.broadcast_to(p, (Z, 4, TILE)).astype(jnp.int32) for p in (power, ec[...])]
        qz[group] = jnp.concatenate([code] + powers, axis=1).astype(jnp.int16)
        for k in range(Z - 1):
            zd = target(k)
            slot = lax.rem(z - zd + Z, Z) - 1
            copy = remote(
                qz.at[group, zd], zr.at[group, slot], zl_s.at[group, k], zl_r.at[group, slot], place_of(zd)
            )
            copy.start()
            ladder_sends.append(copy)

    pick(0, range(GI))
    multiply(0)
    pick(1, range(4))
    scatter(0)
    pick(1, range(4, GI))
    multiply(1)
    for copy in gathers:
        copy.wait_send()
    scatter(1)

    cycle = rc[z]
    for dz in range(1, Z):
        remote(qc.at[0], zc.at[dz - 1], zc_s.at[0], zc_r.at[dz - 1], column(-dz)).wait_recv()
    for copy in cycle_sends:
        copy.wait_send()

    lane = lax.broadcasted_iota(jnp.int32, (GI, TILE), 1)
    blocks = []
    for group in range(2):
        total = rz[group, z]
        for dz in (1, 11, 2, 10, 3, 9, 4, 8, 5, 7, 6):
            remote(
                qz.at[group, 0], zr.at[group, dz - 1], zl_s.at[group, 0], zl_r.at[group, dz - 1], column(-dz)
            ).wait_recv()
            received = zr[group, dz - 1].astype(jnp.int32).astype(F32)
            total = total + decode(received[:24, :], received[24:25, :])
            if group == 0:
                cycle = cycle + decode(zc[dz - 1].astype(jnp.int32).astype(F32), received[28:29, :])
        r1[:24, :] = total
        r1[24:, :] = pltpu.roll(total[16:, :], 64, 1)
        flipped = jnp.concatenate(
            [
                jnp.transpose(jnp.concatenate([r1[pl.ds(16 * k + b, 4, stride=4), :] for b in range(4)], axis=0))
                for k in range(2)
            ],
            axis=0,
        )
        pieces = [jnp.zeros((GI, TILE), F32) for _ in range(4)]
        for j in range(J):
            block = jnp.concatenate(
                [flipped[j * GI : (j + 1) * GI, :], jnp.zeros((GI, TILE - 16), F32)], axis=1
            )
            block = pltpu.roll(block, 4 * j, 1)
            for b in range(4):
                low = 4 * (j + b)
                pieces[b] = jnp.where((lane >= low) & (lane < low + 4), block, pieces[b])
        for b in range(4):
            piece = pieces[b] if b == 0 else pltpu.roll(pieces[b], TILE - 4 * b, 1)
            w2[pl.ds(b, GI, stride=4), :] = piece
        w3[group] = w2[...].reshape(GI, 4, TILE)
        for il in sorted(range(GI), key=lambda il: -hops(GROUPS[group][il])):
            dy, dx = GROUPS[group][il]
            if (dy, dx) == (0, 0):
                own = pltpu.make_async_copy(w3.at[group, il], zz.at[t], self_sem)
                own.start()
                own.wait()
                continue
            slot = dy * X + dx
            copy = remote(w3.at[group, il], zz.at[t], a2a_s.at[slot], a2a_r.at[t], plane(dx, dy))
            copy.start()
            blocks.append(copy)
    for copy in ladder_sends:
        copy.wait_send()
    for dx, dy in others:
        src = plane(dx, dy)["tensor"]
        remote(w3.at[0, 0], zz.at[src], a2a_s.at[0], a2a_r.at[src], plane(dx, dy)).wait_recv()
    final = jnp.transpose(zz[...].reshape(PLANE * 4, TILE))
    out[...] = (final[: J * 4, :] + cycle).astype(BF16)
    for copy in blocks:
        copy.wait_send()


def body(amplitudes, pair_mask, tile_mask, cycle_integrals, ladder_integrals):
    w = jnp.transpose(cycle_integrals, (0, 2, 1, 3))
    g = jnp.transpose(ladder_integrals, (0, 2, 3, 1)).reshape(CW, AB, TILE)
    smem = pl.BlockSpec(memory_space=pltpu.SMEM)
    anywhere = pl.BlockSpec(memory_space=pl.ANY)
    dma = pltpu.SemaphoreType.DMA
    out = pl.pallas_call(
        kernel,
        out_shape=jax.ShapeDtypeStruct((J * 4, TILE), BF16),
        in_specs=[smem, smem, anywhere, anywhere, anywhere],
        out_specs=pl.BlockSpec(memory_space=pltpu.VMEM),
        scratch_shapes=[
            pltpu.VMEM((J, WIN, TILE), BF16),
            pltpu.VMEM((WIN, J * TILE), BF16),
            pltpu.VMEM((J, J, TILE, TILE), BF16),
            pltpu.VMEM((AB, CW * TILE), BF16),
            pltpu.VMEM((PLANE, J * CW, TILE), BF16),
            pltpu.VMEM((2, CW * GC, TILE), F32),
            pltpu.VMEM((2, GC, CW * TILE), BF16),
            pltpu.VMEM((2, Z, J * 4, TILE), F32),
            pltpu.VMEM((Z, J * 4, TILE), F32),
            pltpu.VMEM((Z, J * 4, TILE), jnp.int16),
            pltpu.VMEM((Z, 1, TILE), F32),
            pltpu.VMEM((Z - 1, J * 4, TILE), jnp.int16),
            pltpu.VMEM((2, 2, Z, 24, TILE), F32),
            pltpu.VMEM((2, Z, 24, TILE), F32),
            pltpu.VMEM((2, Z, 32, TILE), jnp.int16),
            pltpu.VMEM((2, Z - 1, 32, TILE), jnp.int16),
            pltpu.VMEM((32, TILE), F32),
            pltpu.VMEM((GI * 4, TILE), F32),
            pltpu.VMEM((2, GI, 4, TILE), F32),
            pltpu.VMEM((PLANE, 4, TILE), F32),
            dma((1 + CW,)), dma((J // 2,)), dma((PLANE,)), dma((PLANE,)), dma((3,)), dma((3,)),
            dma((Z - 1,)), dma((Z - 1,)), dma((2, Z - 1)), dma((2, Z - 1)), dma((PLANE,)), dma((PLANE,)),
            dma, pltpu.SemaphoreType.REGULAR((3,)),
        ],
        compiler_params=pltpu.CompilerParams(
            collective_id=0, has_side_effects=True, vmem_limit_bytes=60 * 2**20
        ),
    )(pair_mask, tile_mask.reshape(1, -1), amplitudes[0], w, g)
    return out.reshape(1, J, 4, TILE)


def solution(mesh):
    in_specs = (
        P("tensor", None, None, "contract"),
        P("tensor", None),
        P(),
        P(None, "contract", None, None),
        P(None, "contract", None, "tensor"),
    )
    out_specs = P("tensor", None, "contract", None)
    return jax.shard_map(body, mesh=mesh, in_specs=in_specs, out_specs=out_specs, check_vma=False)
```
